32 devices in a mesh: seq: 8 (over z, y), tensor: 4 (over x, core).
Axes of the slice: x: 2, y: 2, z: 4, core: 2. Of those that a mesh axis runs over, the one named last changes fastest.
Arguments:
- tokens: bfloat16 [8192, 1280], P('seq'), may hold values from -6 to 6
- cotangent: bfloat16 [8192, 1280], P(('seq', 'tensor')), may hold values from -6 to 6
- lengths: int32 [1, 14], replicated, may hold values from 1 to 2048, as said below
- qkv: float32 [3, 1280, 1280], P(None, 'seq', 'tensor'), may hold values from -0.15625 to 0.15625
- out_proj: float32 [1280, 1280], P('seq', 'tensor'), may hold values from -1 to 1
- mlp: float32 [2, 1280, 1280], P(None, 'seq', 'tensor'), may hold values from -0.15625 to 0.15625
- gains: float32 [2, 1280], replicated, may hold values from 0.5 to 1.5
- query_scale: float32 [80], replicated, may hold values from -1 to 1.5
- row_second: float32 [6, 1280], P(None, 'seq'), as said below
- col_second: float32 [6, 1280], P(None, 'tensor'), as said below
- gain_second: float32 [2, 1280], P(None, 'seq'), may hold values from 819.2 to 16384
- scale_second: float32 [80], replicated, may hold values from 6553.6 to 131072
Outputs:
- result: float32 [8192, 1280], P(('seq', 'tensor'))
- tokens_grad: float32 [8192, 1280], P(('seq', 'tensor'))
- qkv_grad: float32 [3, 1280, 1280], P(None, 'seq', 'tensor')
- out_proj_grad: float32 [1280, 1280], P('seq', 'tensor')
- mlp_grad: float32 [2, 1280, 1280], P(None, 'seq', 'tensor')
- gains_grad: float32 [2, 1280], P(None, 'seq')
- scale_grad: float32 [80], replicated
- qkv_new: float32 [3, 1280, 1280], P(None, 'seq', 'tensor')
- out_proj_new: float32 [1280, 1280], P('seq', 'tensor')
- mlp_new: float32 [2, 1280, 1280], P(None, 'seq', 'tensor')
- gains_new: float32 [2, 1280], P(None, 'seq')
- scale_new: float32 [80], replicated
- row_new: float32 [6, 1280], P(None, 'seq')
- col_new: float32 [6, 1280], P(None, 'tensor')
- update_rms: float32 [6], replicated
- gain_second_new: float32 [2, 1280], P(None, 'seq')
- scale_second_new: float32 [80], replicated
The draws below stay inside these ranges and needn't reach their ends.
Inputs may be any that keep to these rules, and one draw needn't show every extreme that they name: The row lists the 14 document lengths of the packed sequence in order; they sum to 7680, and the last 512 positions are padding. The first document has exactly 2048 tokens; after it, each block of 1024 tokens holds at least two document ends, none at a multiple of 1024. `row_second`: positive statistics. `col_second`: positive statistics.
All inputs are finite; a program needn't handle non-finite values.
Results may differ from the reference program's by a relative error of at most 0.012.
The reference program's roundings to bfloat16 on the way count: a program that leaves them out, or rounds other values in their place, can miss the bound.
Values may be sent and summed in bfloat16 or wider, within the bound.
No kernel may reach another device: no remote copies, remote signals or barrier semaphores. Data moves between devices by JAX's collectives and lax.ppermute only.
A program may use at most 128 MiB of HBM per device.

```python
import math
import jax
import jax.numpy as jnp
from jax import lax

D = 1280
HEADS = 16
HD = 80
FF = 1280
TOK_DEV = 1024
WINDOW = 1024
QB = 512
PAD = 512
SEQ_LEN = 8192
TOKENS = 8192
MOST = 2048
DOCS = 14


MATRIX_LEVELS = (0.5, 0.5, 0.3, 0.01, 0.3, 0.3)


def draw_lengths(key, part):
    regions = (DOCS - 2) // 2
    key_first = jax.random.fold_in(key, 11)
    key_second = jax.random.fold_in(key, 12)
    final = jnp.arange(regions, dtype=jnp.int32) == regions - 1
    upper = jnp.where(final, TOK_DEV - PAD - 1, TOK_DEV - 1).astype(jnp.int32)
    first = jax.random.randint(key_first, (regions,), 1, upper + 1).astype(jnp.int32)
    second = jax.random.randint(key_second, (regions,), 1, upper).astype(jnp.int32)
    second = second + (second >= first).astype(jnp.int32)
    starts = MOST + TOK_DEV * jnp.arange(regions, dtype=jnp.int32)
    lower_cut = starts + jnp.minimum(first, second)
    upper_cut = starts + jnp.maximum(first, second)
    cuts = jnp.stack([lower_cut, upper_cut], axis=1).reshape(-1)
    points = jnp.concatenate([jnp.array([0, MOST], jnp.int32), cuts, jnp.array([TOKENS - PAD], jnp.int32)])
    return (points[1:] - points[:-1]).reshape(1, DOCS).astype(jnp.int32)


def level_draw(key, columns):
    levels = jnp.array(MATRIX_LEVELS, jnp.float32)[:, None] * TOKENS
    rise = jnp.log(4.0)
    ramp = jnp.arange(columns, dtype=jnp.float32) / (columns - 1.0)
    jitter = jax.random.uniform(key, (6, columns), jnp.float32, jnp.log(0.8), jnp.log(1.25))
    return (levels * jnp.exp(rise * ramp[None, :] + jitter)).astype(jnp.float32)


def draw_row_second(key, part):
    return level_draw(jax.random.fold_in(key, 21), D)


def draw_col_second(key, part):
    return level_draw(jax.random.fold_in(key, 22), FF)


def shard_levels(stream_key, extent, shards, smallest, high):
    def one(axis_at, parts):
        draws = jax.random.uniform(jax.random.fold_in(jax.random.fold_in(stream_key, 6), axis_at), (parts,), jnp.float32, smallest / len(shards), high / len(shards))
        return jnp.repeat(jnp.exp(draws), extent[axis_at] // parts).reshape((-1,) + (1,) * (len(extent) - axis_at - 1))

    factor_of = one(*shards[0])
    for cut in shards[1:]:
        factor_of = factor_of * one(*cut)
    return factor_of


def gaussian(key, extent, width, limit, shards=(), kind=jnp.bfloat16):
    gain = shard_levels(key, extent, shards, -0.22, 0.18) if shards else 1.0
    values = jax.random.normal(key, extent, jnp.float32) * width * gain
    return jnp.minimum(jnp.maximum(values, -limit), limit).astype(kind)


def setup_inputs(seed: int = 0) -> dict:
    key_list = jax.random.split(jax.random.key(seed), 13)
    tokens = gaussian(key_list[0], (TOKENS, D), 1.0, 6.0, ((0, 8),))
    cotangent = gaussian(key_list[1], (TOKENS, D), 1.0, 6.0, ((0, 32),))
    lengths = draw_lengths(jax.random.fold_in(key_list[12], 71), 0)
    qkv = gaussian(key_list[3], (3, D, HEADS * HD), D ** -0.5, 0.15625, ((1, 8), (2, 4)), jnp.float32)
    out_proj = gaussian(key_list[4], (D, HEADS * HD), (HEADS * HD // 32) ** -0.5, 1.0, ((0, 8), (1, 4)), jnp.float32)
    mlp = gaussian(key_list[5], (2, D, FF), D ** -0.5, 0.15625, ((1, 8), (2, 4)), jnp.float32)
    gains = jnp.clip(1.0 + 0.1 * jax.random.normal(key_list[6], (2, D), jnp.float32), 0.5, 1.5)
    query_scale = jnp.clip(jax.random.uniform(key_list[7], (HD,), jnp.float32, -1.0, 1.5), -1.0, 1.5)
    row_second = draw_row_second(jax.random.fold_in(key_list[12], 71), 0)
    col_second = draw_col_second(jax.random.fold_in(key_list[12], 71), 0)
    gain_second = jnp.clip(jnp.exp(math.log(16384.0) - 2.9957323 * jax.random.uniform(key_list[10], (2, D), jnp.float32) ** shard_levels(key_list[10], (2, D), ((1, 8),), -0.2, 0.2)), 819.2, 16384.0)
    scale_second = jnp.clip(jnp.exp(jax.random.uniform(key_list[11], (HD,), jnp.float32, math.log(6553.6), math.log(131072.0))), 6553.6, 131072.0)
    return dict(tokens=tokens, cotangent=cotangent, lengths=lengths, qkv=qkv, out_proj=out_proj, mlp=mlp, gains=gains, query_scale=query_scale, row_second=row_second, col_second=col_second, gain_second=gain_second, scale_second=scale_second)


EPSILON = 1e-06
LOG_BASE = 1.442695
BETA_TWO = 0.5
STEP_RATE = 0.3
CLIP_LEVEL = 0.1
VECTOR_RATE = 0.3
NEGATIVE = -1e+30
HIGHEST = lax.Precision.HIGHEST

@jax.custom_vjp
def low(v):
    return lax.optimization_barrier(v.astype(jnp.bfloat16)).astype(jnp.float32)

@jax.custom_vjp
def low_back(v):
    return v

def low_keep(v):
    return (low(v), None)

def low_pass(kept, grad):
    return (grad,)

def back_keep(v):
    return (v, None)

def back_low(kept, grad):
    return (low(grad),)
low.defvjp(low_keep, low_pass)
low_back.defvjp(back_keep, back_low)

def matmul(left, right):
    return jnp.dot(left, right, precision=HIGHEST, preferred_element_type=jnp.float32)

def rms_scale(values):
    return values * lax.rsqrt(lax.optimization_barrier(jnp.mean(values * values, axis=-1, keepdims=True)) + EPSILON)

def label_table(lengths, places):
    ends = jnp.cumsum(lengths, axis=1).astype(jnp.int32)
    sequence = jnp.floor_divide(places, SEQ_LEN).astype(jnp.int32)
    offset = places - sequence * SEQ_LEN
    picked = ends[jnp.clip(sequence, 0, lengths.shape[0] - 1)]
    docnum = lax.optimization_barrier(jnp.sum((picked <= offset[:, None]).astype(jnp.int32), axis=1)).astype(jnp.int32)
    return (sequence * (DOCS + 1) + docnum, (docnum == DOCS).astype(jnp.int32))

def attend(queries, key_rows, value_rows, labels, padded):
    count_rows = queries.shape[0]
    q_heads = queries.reshape(count_rows, HEADS, HD)
    zeros_rim = jnp.zeros((WINDOW, HEADS, HD), jnp.float32)
    k_heads = jnp.concatenate([zeros_rim, key_rows.reshape(count_rows, HEADS, HD)], axis=0)
    v_heads = jnp.concatenate([zeros_rim, value_rows.reshape(count_rows, HEADS, HD)], axis=0)

    def block(begin):
        q_block = lax.dynamic_slice_in_dim(q_heads, begin, QB, 0)
        k_block = lax.dynamic_slice_in_dim(k_heads, begin, QB + WINDOW, 0)
        v_block = lax.dynamic_slice_in_dim(v_heads, begin, QB + WINDOW, 0)
        q_place = begin + WINDOW + jnp.arange(QB, dtype=jnp.int32)
        k_place = begin + jnp.arange(QB + WINDOW, dtype=jnp.int32)
        q_label = lax.dynamic_slice_in_dim(labels, begin + WINDOW, QB, 0)
        k_label = lax.dynamic_slice_in_dim(labels, begin, QB + WINDOW, 0)
        k_pad = lax.dynamic_slice_in_dim(padded, begin, QB + WINDOW, 0)
        before = k_place[None, :] <= q_place[:, None]
        inside = q_place[:, None] - k_place[None, :] < WINDOW
        same_doc = (q_label[:, None] == k_label[None, :]) & (k_pad[None, :] == 0)
        allowed = before & inside & (same_doc | (q_place[:, None] == k_place[None, :]))
        scores = low_back(jnp.einsum('qhd,khd->hqk', q_block, k_block, precision=HIGHEST))
        scores = jnp.where(allowed[None], scores, NEGATIVE)
        top_score = lax.optimization_barrier(jnp.max(scores, axis=-1, keepdims=True))
        weights = jnp.exp(scores - top_score)
        probs = weights / lax.optimization_barrier(jnp.sum(weights, axis=-1, keepdims=True))
        return jnp.einsum('hqk,khd->qhd', low(probs), v_block, precision=HIGHEST)
    begins = jnp.arange(0, count_rows, QB, dtype=jnp.int32)
    mixed = lax.map(jax.checkpoint(block), begins)
    return mixed.reshape(count_rows, HEADS * HD)

def reference(tokens, cotangent, lengths, qkv, out_proj, mlp, gains, query_scale, row_second, col_second, gain_second, scale_second):
    places = jnp.arange(-WINDOW, TOKENS, dtype=jnp.int32)
    labels, padded = label_table(lengths, places)

    def forward(x_full, w_qkv, w_out, w_mlp, gain_pair, scale_raw):
        h_one = low(rms_scale(x_full) * gain_pair[0])
        proj_q = low_back(matmul(h_one, low(w_qkv[0])))
        key_rows = low_back(low(matmul(h_one, low(w_qkv[1]))))
        value_rows = low_back(low(matmul(h_one, low(w_qkv[2]))))
        scale_cols = jnp.tile(jax.nn.softplus(scale_raw) * (LOG_BASE / math.sqrt(HD)), HEADS)
        queries = low(proj_q * scale_cols)
        context = low_back(low(attend(queries, key_rows, value_rows, labels, padded)))
        attn = low_back(matmul(context, low(w_out).T))
        mid = x_full + attn
        h_two = low(rms_scale(mid) * gain_pair[1])
        pre_act = low_back(matmul(h_two, low(w_mlp[0])))
        hidden = low(jax.nn.silu(pre_act))
        return mid + low_back(matmul(hidden, low(w_mlp[1]).T))
    x_full = tokens.astype(jnp.float32)
    result, pull = jax.vjp(forward, x_full, qkv, out_proj, mlp, gains, query_scale)
    tokens_grad, qkv_grad, out_grad, mlp_grad, gains_grad, scale_grad = pull(cotangent.astype(jnp.float32))
    grads = jnp.concatenate([qkv_grad, out_grad[None], mlp_grad], axis=0)
    weights_old = jnp.concatenate([qkv, out_proj[None], mlp], axis=0)
    squares = grads * grads
    row_new = BETA_TWO * row_second + (1.0 - BETA_TWO) * lax.optimization_barrier(jnp.mean(squares, axis=2))
    col_new = BETA_TWO * col_second + (1.0 - BETA_TWO) * lax.optimization_barrier(jnp.mean(squares, axis=1))
    row_mean = lax.optimization_barrier(jnp.mean(row_new, axis=1))
    update = grads * lax.rsqrt(row_new[:, :, None] * col_new[:, None, :] / row_mean[:, None, None])
    update_rms = jnp.sqrt(lax.optimization_barrier(jnp.mean(update * update, axis=(1, 2))))
    fresh = weights_old - STEP_RATE * update / jnp.maximum(1.0, update_rms / CLIP_LEVEL)[:, None, None]
    gain_second_new = BETA_TWO * gain_second + (1.0 - BETA_TWO) * gains_grad * gains_grad
    gains_new = gains - VECTOR_RATE * gains_grad * lax.rsqrt(gain_second_new)
    scale_second_new = BETA_TWO * scale_second + (1.0 - BETA_TWO) * scale_grad * scale_grad
    scale_new = query_scale - VECTOR_RATE * scale_grad * lax.rsqrt(scale_second_new)
    return (result, tokens_grad, qkv_grad, out_grad, mlp_grad, gains_grad, scale_grad, fresh[:3], fresh[3], fresh[4:], gains_new, scale_new, row_new, col_new, update_rms, gain_second_new, scale_second_new)
```

```python
import functools
import math

import jax
import jax.numpy as jnp
from jax import lax
from jax.experimental import pallas as pl
from jax.experimental.pallas import tpu as pltpu
from jax.sharding import PartitionSpec as P

HD = 80
WINDOW = 1024
BLOCK = 256
SPAN = WINDOW + BLOCK
LANES = 128

EPSILON = 1e-06
LOG_BASE = 1.442695
BETA_TWO = 0.5
STEP_RATE = 0.3
CLIP_LEVEL = 0.1
VECTOR_RATE = 0.3
NEGATIVE = -1e30
SCALE_ROOT = LOG_BASE / math.sqrt(HD)
VMEM_LIMIT = 56 * 1024 * 1024

bf16 = jnp.bfloat16
f32 = jnp.float32


def dot(left, right, dims):
    return lax.dot_general(left, right, (dims, ((), ())), preferred_element_type=f32)


def vmem_call(body, outs, scratch, flops, *args):
    size = sum(math.prod(a.shape) * a.dtype.itemsize for a in (*args, *outs))
    space = pl.BlockSpec(memory_space=pltpu.VMEM)
    return pl.pallas_call(
        body,
        out_shape=outs,
        in_specs=[space] * len(args),
        out_specs=[space] * len(outs),
        scratch_shapes=scratch,
        compiler_params=pltpu.CompilerParams(vmem_limit_bytes=VMEM_LIMIT),
        cost_estimate=pl.CostEstimate(flops=int(flops), bytes_accessed=size, transcendentals=0),
    )(*args)


def hop(value, axis, flip):
    peers = lax.axis_size(axis)
    return lax.ppermute(value, axis, [(i, i ^ flip) for i in range(peers)])


def after(value, *earlier):
    return lax.optimization_barrier((value, *earlier))[0]


def put(table, piece, row):
    return lax.dynamic_update_slice_in_dim(table, piece, row, 0)


def outer_pieces(shard):
    peers = lax.axis_size("seq")
    return [shard] + [hop(shard, "seq", f) for f in range(2, peers, 2)]


def pair_up(piece):
    other = hop(piece, "seq", 1)
    low = lax.axis_index("seq") % 2 == 0
    return jnp.concatenate([jnp.where(low, piece, other), jnp.where(low, other, piece)], axis=0)


def assemble(pairs):
    rows, cols = pairs[0].shape
    outer = lax.axis_index("seq") // 2
    table = jnp.zeros((rows * len(pairs), cols), pairs[0].dtype)
    for f, pair in enumerate(pairs):
        table = put(table, pair, (outer ^ f) * rows)
    return table


def scatter_seq(part):
    peers, here = lax.axis_size("seq"), lax.axis_index("seq")
    full, cols = part.shape
    rows = full // peers
    pairs = part.reshape(peers // 2, 2, rows, cols)
    low = here % 2
    send = lax.dynamic_index_in_dim(pairs, 1 - low, 1, keepdims=False)
    keep = lax.dynamic_index_in_dim(pairs, low, 1, keepdims=False)
    half = keep.astype(f32) + hop(send.astype(bf16), "seq", 1).astype(f32)
    pick = lambda f: lax.dynamic_index_in_dim(half, (here // 2) ^ f, 0, keepdims=False)
    total = pick(0)
    for f in range(1, peers // 2):
        total = total + hop(pick(f).astype(bf16), "seq", 2 * f).astype(f32)
    return total


def spread(payload, axis):
    peers = lax.axis_size(axis)
    return lax.all_to_all(
        jnp.broadcast_to(payload, (peers, *payload.shape)), axis, split_axis=0, concat_axis=0
    )


def packed(*values):
    flat = jnp.concatenate([v.reshape(-1) for v in values])
    size = -(-flat.shape[0] // 1024) * 1024
    return jnp.pad(flat, (0, size - flat.shape[0])).reshape(size // 128, 128)


def unpacked(table, *shapes):
    flat, out, at = table.reshape(-1), [], 0
    for shape in shapes:
        size = math.prod(shape)
        out.append(flat[at : at + size].reshape(shape))
        at += size
    return out


def head_of(rows, h):
    zeros = jnp.zeros((rows.shape[0], LANES - HD), rows.dtype)
    return jnp.concatenate([rows[:, h * HD : (h + 1) * HD], zeros], axis=1)


def attend_kernel(heads, h_ref, w_ref, sc_ref, lo_ref, q_ref, k_ref, v_ref, c_ref, lse_ref, kh, vt, bias):
    cols = heads * HD
    rows = q_ref.shape[0]
    for i in range(h_ref.shape[0] // BLOCK):
        at = pl.ds(i * BLOCK, BLOCK)
        proj = dot(h_ref[at, :], w_ref[...], ((1,), (0,)))
        if i * BLOCK >= WINDOW:
            q_ref[pl.ds(i * BLOCK - WINDOW, BLOCK), :] = (proj[:, :cols] * sc_ref[...]).astype(bf16)
        k_rows = proj[:, cols : 2 * cols].astype(bf16)
        v_rows = proj[:, 2 * cols :].astype(bf16)
        k_ref[at, :] = k_rows
        v_ref[at, :] = v_rows
        vt[:, at] = v_rows.T
        for h in range(heads):
            kh[h, at, :] = head_of(k_rows, h)

    def block(b, carry):
        q0 = pl.multiple_of(b * BLOCK, BLOCK)
        k_place = q0 + lax.broadcasted_iota(jnp.int32, (SPAN, BLOCK), 0)
        q_place = q0 + WINDOW + lax.broadcasted_iota(jnp.int32, (SPAN, BLOCK), 1)
        seen = (k_place >= lo_ref[:, pl.ds(q0, BLOCK)]) & (k_place <= q_place)
        bias[...] = jnp.where(seen, 0.0, NEGATIVE)
        q_rows = q_ref[pl.ds(q0, BLOCK), :]
        mixed = []
        for h in range(heads):
            q_head = head_of(q_rows, h)
            s = dot(kh[h, pl.ds(q0, SPAN), :], q_head, ((1,), (1,))) + bias[...]
            top = jnp.max(s, axis=0, keepdims=True)
            p = jnp.exp(s - top)
            total = jnp.sum(p, axis=0, keepdims=True)
            part = dot(vt[h * HD : (h + 1) * HD, pl.ds(q0, SPAN)], p.astype(bf16), ((1,), (0,)))
            mixed.append((part / total).T)
            lse_ref[pl.ds(h, 1), pl.ds(q0, BLOCK)] = top + jnp.log(total)
        c_ref[pl.ds(q0, BLOCK), :] = jnp.concatenate(mixed, axis=1).astype(bf16)
        return carry

    lax.fori_loop(0, rows // BLOCK, block, 0)


def attend_back_kernel(
    heads, q_ref, k_ref, v_ref, g_ref, sc_ref, lo_ref, lse_ref, dq_ref, dkv_ref, part_ref, kh, vh, kt, dk, dv, bias
):
    rows = q_ref.shape[0]
    kt[...] = k_ref[...].T
    for h in range(heads):
        kh[h] = head_of(k_ref[...], h)
        vh[h] = head_of(v_ref[...], h)
    dk[...] = jnp.zeros_like(dk)
    dv[...] = jnp.zeros_like(dv)
    part_ref[...] = jnp.zeros_like(part_ref)

    def block(b, carry):
        q0 = pl.multiple_of(b * BLOCK, BLOCK)
        at, keys = pl.ds(q0, BLOCK), pl.ds(q0, SPAN)
        k_place = q0 + lax.broadcasted_iota(jnp.int32, (SPAN, BLOCK), 0)
        q_place = q0 + WINDOW + lax.broadcasted_iota(jnp.int32, (SPAN, BLOCK), 1)
        seen = (k_place >= lo_ref[:, at]) & (k_place <= q_place)
        bias[...] = jnp.where(seen, 0.0, NEGATIVE)
        q_rows, g_rows = q_ref[at, :], g_ref[at, :]
        grads = []
        for h in range(heads):
            q_head = head_of(q_rows, h)
            g_head = head_of(g_rows, h)
            s = dot(kh[h, keys, :], q_head, ((1,), (1,))) + bias[...]
            p = jnp.exp(s - lse_ref[pl.ds(h, 1), at])
            dp = dot(vh[h, keys, :], g_head, ((1,), (1,)))
            inner = jnp.sum(p * dp, axis=0, keepdims=True)
            ds = (p * (dp - inner)).astype(bf16)
            dv[h, keys, :] += dot(p.astype(bf16), g_head, ((1,), (0,)))
            dk[h, keys, :] += dot(ds, q_head, ((1,), (0,)))
            grads.append(dot(kt[h * HD : (h + 1) * HD, keys], ds, ((1,), (0,))).T)
        grad = jnp.concatenate(grads, axis=1)
        part_ref[...] += jnp.sum(grad * q_rows.astype(f32), axis=0, keepdims=True)
        dq_ref[at, :] = (grad * sc_ref[...]).astype(bf16)
        return carry

    lax.fori_loop(0, rows // BLOCK, block, 0)
    for i in range(k_ref.shape[0] // BLOCK):
        at = pl.ds(i * BLOCK, BLOCK)
        for j, table in enumerate((dk, dv)):
            dkv_ref[j, at, :] = jnp.concatenate(
                [table[h, at, :HD] for h in range(heads)], axis=1
            ).astype(bf16)


def share_kernel(peers, *refs):
    ctx, mats = refs[:peers], refs[peers : 2 * peers]
    x_ref, cot_ref, gain_ref = refs[2 * peers : 2 * peers + 3]
    outs = refs[2 * peers + 3 :]
    res_ref, gmid_ref, part_ref, h2_ref, gm_ref, hid_ref, gpre_ref = outs[:7]
    gctx = outs[7 : 7 + peers]
    w_out, w_in, w_back = outs[7 + peers :]
    cols = ctx[0].shape[1]
    for r, m in enumerate(mats):
        for j, w in enumerate((w_out, w_in, w_back)):
            w[:, r * cols : (r + 1) * cols] = m[:, j * cols : (j + 1) * cols]
    gain = gain_ref[...]
    mixed = jnp.concatenate([c[...] for c in ctx], axis=1)
    mid = x_ref[...].astype(f32) + dot(mixed, w_out[...], ((1,), (1,)))
    factor = lax.rsqrt(jnp.mean(mid * mid, axis=-1, keepdims=True) + EPSILON)
    normed = mid * factor
    h2 = (normed * gain).astype(bf16)
    h2_ref[...] = h2
    cot = cot_ref[...]
    pre = dot(h2, w_in[...], ((1,), (0,)))
    g_hid = dot(cot, w_back[...], ((1,), (0,)))
    sig = 1.0 / (1.0 + jnp.exp(-pre))
    hidden = (pre * sig).astype(bf16)
    g_pre = (g_hid * sig * (1.0 + pre * (1.0 - sig))).astype(bf16)
    for r in range(peers):
        hid_ref[r] = hidden[:, r * cols : (r + 1) * cols]
        gpre_ref[r] = g_pre[:, r * cols : (r + 1) * cols]
    res_ref[...] = mid + dot(hidden, w_back[...], ((1,), (1,)))
    g_h2 = dot(g_pre, w_in[...], ((1,), (1,)))
    part_ref[...] = jnp.sum(g_h2 * normed, axis=0, keepdims=True)
    scaled = g_h2 * gain
    back = factor * (scaled - normed * jnp.mean(scaled * normed, axis=-1, keepdims=True))
    g_mid = cot.astype(f32) + back
    gmid_ref[...] = g_mid
    gm = g_mid.astype(bf16)
    gm_ref[...] = gm
    g_mixed = dot(gm, w_out[...], ((1,), (0,))).astype(bf16)
    for r, out in enumerate(gctx):
        out[...] = g_mixed[:, r * cols : (r + 1) * cols]


def share_grads_kernel(peers, *refs):
    ctx = refs[:peers]
    gm_ref, h2_ref, cot_ref, gpre_ref, hid_ref = refs[peers : peers + 5]
    outs = refs[peers + 5 :]
    lefts = (gm_ref[...].T, h2_ref[...].T, cot_ref[...].T)
    split = outs[0].shape[-1]
    for r in range(peers):
        parts = [
            dot(left, right, ((1,), (0,))).astype(bf16)
            for left, right in zip(lefts, (ctx[r][...], gpre_ref[r], hid_ref[r]))
        ]
        whole = jnp.concatenate(parts, axis=1)
        outs[r % 2][r // 2] = whole[:, :split]
        outs[2 + r % 2][r // 2] = whole[:, split:]


def shards(
    tokens,
    cotangent,
    lengths,
    qkv,
    out_proj,
    mlp,
    gains,
    query_scale,
    row_second,
    col_second,
    gain_second,
    scale_second,
):
    n_tensor, n_seq = lax.axis_size("tensor"), lax.axis_size("seq")
    seq_index, ten_index = lax.axis_index("seq"), lax.axis_index("tensor")
    tok_dev, width = tokens.shape
    share = cotangent.shape[0]
    rows_own, cols_own = qkv.shape[1], qkv.shape[2]
    heads = cols_own // HD
    row_first = ten_index * share
    flips = list(range(n_tensor))
    sds = jax.ShapeDtypeStruct

    x_share = lax.dynamic_slice_in_dim(tokens, row_first, share, 0)
    rim_own = lax.ppermute(x_share, "seq", [(i, i + 1) for i in range(n_seq - 1)])

    shard_m = jnp.concatenate([out_proj, mlp[0], mlp[1]], axis=1).astype(bf16)
    shard_qkv = jnp.concatenate([qkv[0], qkv[1], qkv[2]], axis=1).astype(bf16)
    outer_m = outer_pieces(shard_m)
    pairs_m = [pair_up(piece) for piece in outer_m]
    rim_outer = [rim_own] + [hop(rim_own, "tensor", f) for f in flips[2::2]]
    rim_inner = [hop(piece, "tensor", 1) for piece in rim_outer]
    mats = [None] * n_tensor
    mats[0] = assemble(pairs_m)
    for f in flips[2::2]:
        mats[f] = assemble([hop(pair, "tensor", f) for pair in pairs_m])
    for f in flips[::2]:
        mats[f + 1] = hop(mats[f], "tensor", 1)
    outer_q = outer_pieces(after(shard_qkv, outer_m[-1], rim_own))
    w_qkv = assemble([pair_up(piece) for piece in outer_q])

    rim = jnp.zeros((WINDOW + tok_dev, width), bf16)
    rim = put(rim, tokens, WINDOW)
    for f, one, two in zip(flips[::2], rim_outer, rim_inner):
        rim = put(rim, one, (ten_index ^ f) * share)
        rim = put(rim, two, (ten_index ^ f ^ 1) * share)
    x_all = rim.astype(f32)
    factor_all = lax.rsqrt(jnp.mean(x_all * x_all, axis=-1, keepdims=True) + EPSILON)
    h_all = (x_all * factor_all * gains[0]).astype(bf16)

    places = seq_index * tok_dev + jnp.arange(tok_dev, dtype=jnp.int32)
    ends = jnp.cumsum(lengths[0])
    passed = ends[None, :] <= places[:, None]
    doc_start = jnp.max(jnp.where(passed, ends[None, :], 0), axis=1)
    lo = jnp.maximum(places - (WINDOW - 1), doc_start)
    lo = jnp.where(places >= ends[-1], places, lo)
    lo = (lo - (seq_index * tok_dev - WINDOW)).astype(jnp.int32)[None, :]

    factor = jax.nn.softplus(query_scale) * SCALE_ROOT
    scale_cols = jnp.tile(factor, heads)[None, :]
    table = WINDOW + tok_dev
    pair_flops = tok_dev * SPAN * cols_own * 2
    queries, key_rows, value_rows, context, log_totals = vmem_call(
        functools.partial(attend_kernel, heads),
        (
            sds((tok_dev, cols_own), bf16),
            sds((table, cols_own), bf16),
            sds((table, cols_own), bf16),
            sds((tok_dev, cols_own), bf16),
            sds((heads, tok_dev), f32),
        ),
        [
            pltpu.VMEM((heads, table, LANES), bf16),
            pltpu.VMEM((cols_own, table), bf16),
            pltpu.VMEM((SPAN, BLOCK), f32),
        ],
        2 * table * width * 3 * cols_own + 6 * pair_flops,
        h_all,
        w_qkv,
        scale_cols,
        lo,
    )

    def share_of(values, f):
        return lax.dynamic_slice_in_dim(values, (ten_index ^ f) * share, share, 0)

    ctx = [share_of(context, f) for f in flips]
    ctx = [ctx[0]] + [hop(ctx[f], "tensor", f) for f in flips[1:]]
    shape_share = (share, width)
    outs = vmem_call(
        functools.partial(share_kernel, n_tensor),
        (
            sds(shape_share, f32),
            sds(shape_share, f32),
            sds((1, width), f32),
            sds(shape_share, bf16),
            sds(shape_share, bf16),
            sds((n_tensor, share, cols_own), bf16),
            sds((n_tensor, share, cols_own), bf16),
            *[sds((share, cols_own), bf16) for _ in flips],
        ),
        [pltpu.VMEM((width, width), bf16) for _ in range(3)],
        2 * 6 * share * width * width,
        *ctx,
        *mats,
        x_share,
        cotangent,
        gains[1:],
    )
    result, grad_mid, gain_two_grad, h_two, grad_mid_low, hidden, grad_pre = outs[:7]
    gctx = list(outs[7:])
    gctx = [gctx[0]] + [hop(gctx[f], "tensor", f) for f in flips[1:]]
    grad_context = jnp.zeros((tok_dev, cols_own), bf16)
    for f in flips:
        grad_context = put(grad_context, gctx[f], (ten_index ^ f) * share)

    split = -(-3 * cols_own // 256) * 128
    chunks = [sds((n_tensor // 2, width, c), bf16) for c in (split, 3 * cols_own - split)]
    halves = vmem_call(
        functools.partial(share_grads_kernel, n_tensor),
        (chunks[0], chunks[0], chunks[1], chunks[1]),
        [],
        2 * 3 * share * width * width,
        *ctx,
        grad_mid_low,
        h_two,
        cotangent,
        grad_pre,
        hidden,
    )
    own_m = []
    for even, odd in (halves[:2], halves[2:]):
        from_core = hop(odd, "tensor", 1)
        sums = [even[i].astype(f32) + from_core[i].astype(f32) for i in range(n_tensor // 2)]
        grad_m = sums[0]
        for i in range(1, n_tensor // 2):
            grad_m = grad_m + hop(sums[i].astype(bf16), "tensor", 2 * i).astype(f32)
        own_m.append(scatter_seq(grad_m))
    own_m = jnp.concatenate(own_m, axis=1)

    grad_q, grad_kv, scale_raw = vmem_call(
        functools.partial(attend_back_kernel, heads),
        (
            sds((tok_dev, cols_own), bf16),
            sds((2, table, cols_own), bf16),
            sds((1, cols_own), f32),
        ),
        [
            pltpu.VMEM((heads, table, LANES), bf16),
            pltpu.VMEM((heads, table, LANES), bf16),
            pltpu.VMEM((cols_own, table), bf16),
            pltpu.VMEM((heads, table, LANES), f32),
            pltpu.VMEM((heads, table, LANES), f32),
            pltpu.VMEM((SPAN, BLOCK), f32),
        ],
        14 * pair_flops,
        queries,
        key_rows,
        value_rows,
        grad_context,
        scale_cols,
        lo,
        log_totals,
    )
    scale_part = (
        jnp.sum((scale_raw / scale_cols).reshape(heads, HD), axis=0)
        * SCALE_ROOT
        * jax.nn.sigmoid(query_scale)
    )
    grad_w = jnp.concatenate(
        [
            dot(h_all[WINDOW:], grad_q, ((0,), (0,))),
            dot(h_all, grad_kv[0], ((0,), (0,))),
            dot(h_all, grad_kv[1], ((0,), (0,))),
        ],
        axis=1,
    ).astype(bf16)
    own_qkv = scatter_seq(grad_w)

    back = lax.ppermute(grad_kv[:, :WINDOW], "seq", [(i, i - 1) for i in range(1, n_seq)])
    own_kv = grad_kv[:, WINDOW:].astype(f32)
    own_kv = own_kv.at[:, tok_dev - WINDOW :].add(back.astype(f32)).astype(bf16)
    grad_proj = jnp.concatenate([grad_q, own_kv[0], own_kv[1]], axis=1)
    partial_one = dot(grad_proj, w_qkv, ((1,), (1,))).astype(bf16)
    odd_rows = jnp.stack([share_of(partial_one, f + 1) for f in flips[::2]])
    even_rows = [share_of(partial_one, f).astype(f32) for f in flips[::2]]
    from_core_rows = hop(odd_rows, "tensor", 1).astype(f32)
    sums = [rows + from_core_rows[i] for i, rows in enumerate(even_rows)]
    grad_one = sums[0]
    for i in range(1, n_tensor // 2):
        grad_one = grad_one + hop(sums[i].astype(bf16), "tensor", 2 * i).astype(f32)
    x_part = x_share.astype(f32)
    factor_one = lax.rsqrt(jnp.mean(x_part * x_part, axis=-1, keepdims=True) + EPSILON)
    norm_one = x_part * factor_one
    gain_one_grad = jnp.sum(grad_one * norm_one, axis=0)
    scaled = grad_one * gains[0]
    tokens_grad = grad_mid + factor_one * (
        scaled - norm_one * jnp.mean(scaled * norm_one, axis=-1, keepdims=True)
    )

    stacked = jnp.stack(
        [g[:, i * cols_own : (i + 1) * cols_own] for g in (own_qkv, own_m) for i in range(3)]
    )
    squares = stacked * stacked
    col_part = jnp.sum(squares, axis=1)
    row_part = jnp.sum(squares, axis=2)
    seq_sums = jnp.sum(spread(packed(col_part, jnp.sum(row_second, axis=1)), "seq"), axis=0)
    col_square, old_sums = unpacked(seq_sums, (6, cols_own), (6,))
    ten_sums = jnp.sum(spread(packed(row_part, jnp.sum(col_square, axis=1)), "tensor"), axis=0)
    row_square, all_square = unpacked(ten_sums, (6, rows_own), (6,))
    total_cols = cols_own * n_tensor
    row_new = BETA_TWO * row_second + (1.0 - BETA_TWO) * row_square / total_cols
    col_new = BETA_TWO * col_second + (1.0 - BETA_TWO) * col_square / width
    row_mean = (BETA_TWO * old_sums + (1.0 - BETA_TWO) * all_square / total_cols) / width
    update = stacked * lax.rsqrt(
        row_new[:, :, None] * col_new[:, None, :] / row_mean[:, None, None]
    )
    update_part = jnp.sum(update * update, axis=(1, 2))

    gain_part = jnp.stack([gain_one_grad, gain_two_grad[0]])
    gain_part = gain_part.reshape(2, n_seq, rows_own).transpose(1, 0, 2).reshape(n_seq, 2 * rows_own)
    rest = jnp.broadcast_to(jnp.concatenate([scale_part, update_part]), (n_seq, HD + 6))
    last = jnp.concatenate([gain_part, rest], axis=1)
    size = -(-last.shape[1] // 1024) * 1024
    last = jnp.pad(last, ((0, 0), (0, size - last.shape[1]))).reshape(n_seq, 1, size // 128, 128)
    last = jnp.broadcast_to(last, (n_seq, n_tensor, size // 128, 128))
    last = last.reshape(n_seq * n_tensor, size // 128, 128)
    got = lax.all_to_all(last, ("seq", "tensor"), split_axis=0, concat_axis=0)
    gains_grad, scale_grad, update_square = unpacked(
        jnp.sum(got, axis=0), (2, rows_own), (HD,), (6,)
    )
    update_rms = jnp.sqrt(update_square / (width * total_cols))
    weights_old = jnp.concatenate([qkv, out_proj[None], mlp], axis=0)
    fresh = (
        weights_old - STEP_RATE * update / jnp.maximum(1.0, update_rms / CLIP_LEVEL)[:, None, None]
    )
    gains_own = lax.dynamic_slice_in_dim(gains, seq_index * rows_own, rows_own, 1)
    gain_second_new = BETA_TWO * gain_second + (1.0 - BETA_TWO) * gains_grad * gains_grad
    gains_new = gains_own - VECTOR_RATE * gains_grad * lax.rsqrt(gain_second_new)
    scale_second_new = BETA_TWO * scale_second + (1.0 - BETA_TWO) * scale_grad * scale_grad
    scale_new = query_scale - VECTOR_RATE * scale_grad * lax.rsqrt(scale_second_new)
    return (
        result,
        tokens_grad,
        stacked[:3],
        stacked[3],
        stacked[4:],
        gains_grad,
        scale_grad,
        fresh[:3],
        fresh[3],
        fresh[4:],
        gains_new,
        scale_new,
        row_new,
        col_new,
        update_rms,
        gain_second_new,
        scale_second_new,
    )


def solution(mesh):
    return jax.shard_map(
        shards,
        mesh=mesh,
        in_specs=(
            P("seq", None),
            P(("seq", "tensor"), None),
            P(),
            P(None, "seq", "tensor"),
            P("seq", "tensor"),
            P(None, "seq", "tensor"),
            P(),
            P(),
            P(None, "seq"),
            P(None, "tensor"),
            P(None, "seq"),
            P(),
        ),
        out_specs=(
            P(("seq", "tensor"), None),
            P(("seq", "tensor"), None),
            P(None, "seq", "tensor"),
            P("seq", "tensor"),
            P(None, "seq", "tensor"),
            P(None, "seq"),
            P(),
            P(None, "seq", "tensor"),
            P("seq", "tensor"),
            P(None, "seq", "tensor"),
            P(None, "seq"),
            P(),
            P(None, "seq"),
            P(None, "tensor"),
            P(),
            P(None, "seq"),
            P(),
        ),
        check_vma=False,
    )
```

```python
import functools
import math

import jax
import jax.numpy as jnp
from jax import lax
from jax.experimental import pallas as pl
from jax.experimental.pallas import tpu as pltpu
from jax.sharding import PartitionSpec as P

HD = 80
WINDOW = 1024
BLOCK = 256
SPAN = WINDOW + BLOCK
LANES = 128

EPSILON = 1e-06
LOG_BASE = 1.442695
BETA_TWO = 0.5
STEP_RATE = 0.3
CLIP_LEVEL = 0.1
VECTOR_RATE = 0.3
NEGATIVE = -1e30
SCALE_ROOT = LOG_BASE / math.sqrt(HD)
MIB = 1024 * 1024

bf16 = jnp.bfloat16
f32 = jnp.float32


def dot(left, right, dims):
    return lax.dot_general(left, right, (dims, ((), ())), preferred_element_type=f32)


def vmem_call(body, outs, scratch, flops, limit, *args):
    size = sum(math.prod(a.shape) * a.dtype.itemsize for a in (*args, *outs))
    space = pl.BlockSpec(memory_space=pltpu.VMEM)
    scalars = pl.BlockSpec(memory_space=pltpu.SMEM)
    return pl.pallas_call(
        body,
        out_shape=outs,
        in_specs=[scalars if a.ndim == 1 else space for a in args],
        out_specs=[space] * len(outs),
        scratch_shapes=scratch,
        compiler_params=pltpu.CompilerParams(vmem_limit_bytes=limit * MIB),
        cost_estimate=pl.CostEstimate(flops=8 * int(flops), bytes_accessed=size, transcendentals=0),
    )(*args)


def hop(value, axis, flip):
    peers = lax.axis_size(axis)
    return lax.ppermute(value, axis, [(i, i ^ flip) for i in range(peers)])


def after(value, *earlier):
    return lax.optimization_barrier((value, *earlier))[0]


def put(table, piece, row):
    return lax.dynamic_update_slice_in_dim(table, piece, row, 0)


def pair_up(piece):
    other = hop(piece, "seq", 1)
    low = lax.axis_index("seq") % 2 == 0
    return jnp.concatenate([jnp.where(low, piece, other), jnp.where(low, other, piece)], axis=0)


def gather_pairs(shard, first, second):
    peers = lax.axis_size("seq")
    pairs = {}
    for f in range(0, peers // 2, 2):
        pairs[f] = pair_up(after(hop(after(shard, first), "seq", 2 * f), first) if f else shard)
    for f in range(0, peers // 2, 2):
        pairs[f + 1] = hop(after(pairs[f], second(f, pairs)), "seq", 2)
    return pairs


def gather_groups(shard):
    peers = lax.axis_size("seq")
    evens = list(range(0, peers // 2, 2))
    groups = [shard[None]]
    if evens[1:]:
        groups.append(jnp.stack([hop(shard, "seq", 2 * f) for f in evens[1:]]))
    others = [hop(group, "seq", 1) for group in groups]
    groups.append(hop(jnp.concatenate(groups, axis=0), "seq", 2))
    others.append(hop(groups[-1], "seq", 1))
    return groups, others, evens + [f + 1 for f in evens]


def scatter_step(total, left, k):
    at = len(left) - 1 - left.index(k)
    bit = (lax.axis_index("seq") >> k) & 1
    send = lax.dynamic_index_in_dim(total, 1 - bit, at, keepdims=False).astype(bf16)
    return send, lax.dynamic_index_in_dim(total, bit, at, keepdims=False)


def scatter_seq(total, left, order, *earlier):
    left = list(left)
    for k in order:
        send, keep = scatter_step(total, left, k)
        send = after(send, *earlier) if k == order[-1] else send
        left.remove(k)
        came = hop(send, "seq", 1 << k)
        if left:
            total = keep.astype(f32) + came.astype(f32)
    return keep, came


def summed(value, axis):
    flip = 1
    while flip < lax.axis_size(axis):
        value = value + hop(value, axis, flip)
        flip *= 2
    return value


def packed(*values):
    flat = jnp.concatenate([v.reshape(-1) for v in values])
    size = -(-flat.shape[0] // 1024) * 1024
    return jnp.pad(flat, (0, size - flat.shape[0])).reshape(size // 128, 128)


def unpacked(table, *shapes):
    flat, out, at = table.reshape(-1), [], 0
    for shape in shapes:
        size = math.prod(shape)
        out.append(flat[at : at + size].reshape(shape))
        at += size
    return out


def head_of(rows, h):
    zeros = jnp.zeros((rows.shape[0], LANES - HD), rows.dtype)
    return jnp.concatenate([rows[:, h * HD : (h + 1) * HD], zeros], axis=1)


def attend_kernel(heads, counts, *refs):
    n_near, n_rim = counts
    at_ref, tok_ref = refs[:2]
    rims = refs[2 : 2 + n_rim]
    near = refs[2 + n_rim : 2 + n_rim + n_near]
    far = refs[2 + n_rim + n_near : 2 + n_rim + 2 * n_near]
    gain_ref, sc_ref, lo_ref = refs[2 + n_rim + 2 * n_near : 5 + n_rim + 2 * n_near]
    h_ref, q_ref, k_ref, v_ref, c_ref, lse_ref, w_ref, kh, vt, bias = refs[5 + n_rim + 2 * n_near :]
    cols = heads * HD
    rows = q_ref.shape[0]

    low, spot = at_ref[0], 1
    for one, two in zip(near, far):
        for i in range(one.shape[0]):
            at = pl.ds(pl.multiple_of(at_ref[spot], 16), 2 * one.shape[1])
            spot += 1

            @pl.when(low == 0)
            def _():
                w_ref[at, :] = jnp.concatenate([one[i], two[i]], axis=0)

            @pl.when(low == 1)
            def _():
                w_ref[at, :] = jnp.concatenate([two[i], one[i]], axis=0)

    def norm(values):
        values = values.astype(f32)
        factor = lax.rsqrt(jnp.mean(values * values, axis=-1, keepdims=True) + EPSILON)
        return (values * factor * gain_ref[...]).astype(bf16)

    for rim in rims:
        share = rim.shape[0]
        h_ref[pl.ds(pl.multiple_of(at_ref[spot], 16), share), :] = norm(rim[...])
        spot += 1
    for i in range(rows // BLOCK):
        h_ref[WINDOW + i * BLOCK : WINDOW + (i + 1) * BLOCK, :] = norm(
            tok_ref[i * BLOCK : (i + 1) * BLOCK, :]
        )

    for i in range(h_ref.shape[0] // BLOCK):
        at = pl.ds(i * BLOCK, BLOCK)
        proj = dot(h_ref[at, :], w_ref[:, : 3 * cols], ((1,), (0,)))
        if i * BLOCK >= WINDOW:
            q_ref[pl.ds(i * BLOCK - WINDOW, BLOCK), :] = (proj[:, :cols] * sc_ref[...]).astype(bf16)
        k_rows = proj[:, cols : 2 * cols].astype(bf16)
        v_rows = proj[:, 2 * cols :].astype(bf16)
        k_ref[at, :] = k_rows
        v_ref[at, :] = v_rows
        vt[:, at] = v_rows.T
        for h in range(heads):
            kh[h, at, :] = head_of(k_rows, h)

    def block(b, carry):
        q0 = pl.multiple_of(b * BLOCK, BLOCK)
        k_place = q0 + lax.broadcasted_iota(jnp.int32, (SPAN, BLOCK), 0)
        q_place = q0 + WINDOW + lax.broadcasted_iota(jnp.int32, (SPAN, BLOCK), 1)
        seen = (k_place >= lo_ref[:, pl.ds(q0, BLOCK)]) & (k_place <= q_place)
        bias[...] = jnp.where(seen, 0.0, NEGATIVE)
        q_rows = q_ref[pl.ds(q0, BLOCK), :]
        mixed = []
        for h in range(heads):
            q_head = head_of(q_rows, h)
            s = dot(kh[h, pl.ds(q0, SPAN), :], q_head, ((1,), (1,))) + bias[...]
            top = jnp.max(s, axis=0, keepdims=True)
            p = jnp.exp(s - top)
            total = jnp.sum(p, axis=0, keepdims=True)
            part = dot(vt[h * HD : (h + 1) * HD, pl.ds(q0, SPAN)], p.astype(bf16), ((1,), (0,)))
            mixed.append((part / total).T)
            lse_ref[pl.ds(h, 1), pl.ds(q0, BLOCK)] = top + jnp.log(total)
        c_ref[pl.ds(q0, BLOCK), :] = jnp.concatenate(mixed, axis=1).astype(bf16)
        return carry

    lax.fori_loop(0, rows // BLOCK, block, 0)


def attend_back_kernel(heads, n_parts, at_ref, *refs):
    parts = refs[:n_parts]
    q_ref, k_ref, v_ref, sc_ref, lo_ref, lse_ref, h_ref = refs[n_parts : n_parts + 7]
    outs = refs[n_parts + 7 :]
    dq_ref, dkv_ref, part_ref = outs[:3]
    send_ref, keep_ref = outs[3:5]
    kh, vh, kt, ht, g_ref, dk, dv, bias = outs[5:]
    rows, cols = q_ref.shape
    for i, part in enumerate(parts):
        share = part.shape[0]
        g_ref[pl.ds(pl.multiple_of(at_ref[1 + i], 16), share), :] = part[...]
    kt[...] = k_ref[...].T
    for h in range(heads):
        kh[h] = head_of(k_ref[...], h)
        vh[h] = head_of(v_ref[...], h)
    dk[...] = jnp.zeros_like(dk)
    dv[...] = jnp.zeros_like(dv)
    part_ref[...] = jnp.zeros_like(part_ref)

    def block(b, carry):
        q0 = pl.multiple_of(b * BLOCK, BLOCK)
        at, keys = pl.ds(q0, BLOCK), pl.ds(q0, SPAN)
        k_place = q0 + lax.broadcasted_iota(jnp.int32, (SPAN, BLOCK), 0)
        q_place = q0 + WINDOW + lax.broadcasted_iota(jnp.int32, (SPAN, BLOCK), 1)
        seen = (k_place >= lo_ref[:, at]) & (k_place <= q_place)
        bias[...] = jnp.where(seen, 0.0, NEGATIVE)
        q_rows, g_rows = q_ref[at, :], g_ref[at, :]
        grads = []
        for h in range(heads):
            q_head = head_of(q_rows, h)
            g_head = head_of(g_rows, h)
            s = dot(kh[h, keys, :], q_head, ((1,), (1,))) + bias[...]
            p = jnp.exp(s - lse_ref[pl.ds(h, 1), at])
            dp = dot(vh[h, keys, :], g_head, ((1,), (1,)))
            inner = jnp.sum(p * dp, axis=0, keepdims=True)
            ds = (p * (dp - inner)).astype(bf16)
            dv[h, keys, :] += dot(p.astype(bf16), g_head, ((1,), (0,)))
            dk[h, keys, :] += dot(ds, q_head, ((1,), (0,)))
            grads.append(dot(kt[h * HD : (h + 1) * HD, keys], ds, ((1,), (0,))).T)
        grad = jnp.concatenate(grads, axis=1)
        part_ref[...] += jnp.sum(grad * q_rows.astype(f32), axis=0, keepdims=True)
        dq_ref[at, :] = (grad * sc_ref[...]).astype(bf16)
        return carry

    lax.fori_loop(0, rows // BLOCK, block, 0)
    for i in range(k_ref.shape[0] // BLOCK):
        at = pl.ds(i * BLOCK, BLOCK)
        both = [table[h, at, :HD] for table in (dk, dv) for h in range(heads)]
        dkv_ref[at, :] = jnp.concatenate(both, axis=1).astype(bf16)
        ht[:, at] = h_ref[at, :].T
    gw_q = dot(ht[:, WINDOW:], dq_ref[...], ((1,), (0,))).astype(bf16)
    gw_kv = dot(ht[...], dkv_ref[...], ((1,), (0,))).astype(bf16)
    outer, own, padded = send_ref.shape
    zeros = jnp.zeros((2 * outer * own, padded - 3 * cols), bf16)
    whole = jnp.concatenate([gw_q, gw_kv, zeros], axis=1)
    for low in range(2):

        @pl.when(at_ref[0] == low)
        def _():
            for i in range(2 * outer):
                to = keep_ref if i % 2 == low else send_ref
                to[i // 2] = whole[i * own : (i + 1) * own]


def rows_kernel(parts, at_ref, q_ref, kv_ref, w_ref, even_ref, odd_ref):
    cols, width = q_ref.shape[1], w_ref.shape[0]
    share = even_ref.shape[1]
    for f in range(parts):
        at = pl.multiple_of(at_ref[f], 16)
        here = pl.ds(pl.multiple_of(at + WINDOW, 16), share)
        to = odd_ref if f % 2 else even_ref
        grads = jnp.concatenate([q_ref[pl.ds(at, share), :], kv_ref[here, :]], axis=1)
        to[f // 2, :, width:] = dot(grads, w_ref[:, : 3 * cols], ((1,), (1,))).astype(bf16)
        to[f // 2, :, :width] = dot(
            kv_ref[pl.ds(at, share), :], w_ref[:, cols : 3 * cols], ((1,), (1,))
        ).astype(bf16)


def rows_kernel(parts, at_ref, q_ref, kv_ref, w_ref, even_ref, odd_ref):
    cols, width = q_ref.shape[1], w_ref.shape[0]
    share = even_ref.shape[1]
    for f in range(parts):
        at = pl.multiple_of(at_ref[f], 16)
        here = pl.ds(pl.multiple_of(at + WINDOW, 16), share)
        to = odd_ref if f % 2 else even_ref
        grads = jnp.concatenate([q_ref[pl.ds(at, share), :], kv_ref[here, :]], axis=1)
        to[f // 2, :, width:] = dot(grads, w_ref[:, : 3 * cols], ((1,), (1,))).astype(bf16)
        to[f // 2, :, :width] = dot(
            kv_ref[pl.ds(at, share), :], w_ref[:, cols : 3 * cols], ((1,), (1,))
        ).astype(bf16)


def share_kernel(counts, at_ref, *refs):
    peers = len(counts)
    ctx, refs = refs[:peers], refs[peers:]
    mats = [refs[sum(counts[:r]) : sum(counts[: r + 1])] for r in range(peers)]
    refs = refs[sum(counts) :]
    x_ref, cot_ref, gain_ref = refs[:3]
    outs = refs[3:]
    res_ref, gmid_ref, part_ref, rows_ref, even_ref, odd_ref = outs[:6]
    gctx = outs[6 : 6 + peers]
    w_out, w_in, w_back = outs[6 + peers :]
    cols = ctx[0].shape[1]
    for r, pieces in enumerate(mats):
        for i, (m, k) in enumerate((m, k) for m in pieces for k in range(m.shape[0])):
            at = pl.ds(pl.multiple_of(at_ref[i], 16), m.shape[1])
            for j, w in enumerate((w_out, w_in, w_back)):
                w[at, r * cols : (r + 1) * cols] = m[k, :, j * cols : (j + 1) * cols]
    gain = gain_ref[...]
    mixed = jnp.concatenate([c[...] for c in ctx], axis=1)
    mid = x_ref[...].astype(f32) + dot(mixed, w_out[...], ((1,), (1,)))
    factor = lax.rsqrt(jnp.mean(mid * mid, axis=-1, keepdims=True) + EPSILON)
    normed = mid * factor
    h2 = (normed * gain).astype(bf16)
    rows_ref[1] = h2
    cot = cot_ref[...]
    pre = dot(h2, w_in[...], ((1,), (0,)))
    g_hid = dot(cot, w_back[...], ((1,), (0,)))
    sig = 1.0 / (1.0 + jnp.exp(-pre))
    hidden = (pre * sig).astype(bf16)
    g_pre = (g_hid * sig * (1.0 + pre * (1.0 - sig))).astype(bf16)
    for r in range(peers):
        half, to = odd_ref if r % 2 else even_ref, slice(r // 2 * cols, (r // 2 + 1) * cols)
        half[0, :, to] = g_pre[:, r * cols : (r + 1) * cols]
        half[1, :, to] = hidden[:, r * cols : (r + 1) * cols]
    res_ref[...] = mid + dot(hidden, w_back[...], ((1,), (1,)))
    g_h2 = dot(g_pre, w_in[...], ((1,), (1,)))
    part_ref[...] = jnp.sum(g_h2 * normed, axis=0, keepdims=True)
    scaled = g_h2 * gain
    back = factor * (scaled - normed * jnp.mean(scaled * normed, axis=-1, keepdims=True))
    g_mid = cot.astype(f32) + back
    gmid_ref[...] = g_mid
    gm = g_mid.astype(bf16)
    rows_ref[0] = gm
    g_mixed = dot(gm, w_out[...], ((1,), (0,))).astype(bf16)
    for r, out in enumerate(gctx):
        out[...] = g_mixed[:, r * cols : (r + 1) * cols]


def share_grads_kernel(count, at_ref, *refs):
    ctx, ctx_far = refs[:count], refs[count]
    rows_ref, rows_far, even_ref, odd_far, cot_ref, cot_far = refs[count + 1 : count + 7]
    firsts, send_ref, keep_ref = refs[count + 7 : 2 * count + 7], *refs[2 * count + 7 :]
    lefts = [
        jnp.concatenate([one.T, two.T], axis=1)
        for one, two in (
            (rows_ref[0], rows_far[0]),
            (rows_ref[1], rows_far[1]),
            (cot_ref[...], cot_far[...]),
        )
    ]
    half, cols = firsts[0].shape[-1], ctx[0].shape[1]
    zeros = jnp.zeros((firsts[0].shape[0], 2 * half - 3 * cols), bf16)
    pairs, rows = send_ref.shape[1:3]
    for r in range(count):
        to = slice(r * cols, (r + 1) * cols)
        rights = (
            (ctx[r][...], ctx_far[:, to]),
            (even_ref[0, :, to], odd_far[0, :, to]),
            (even_ref[1, :, to], odd_far[1, :, to]),
        )
        parts = [
            dot(left, jnp.concatenate(right, axis=0), ((1,), (0,))).astype(bf16)
            for left, right in zip(lefts, rights)
        ]
        whole = jnp.concatenate([*parts, zeros], axis=1)
        firsts[r][...] = whole[:, :half]
        for bit, (zero, one) in enumerate(((keep_ref, send_ref), (send_ref, keep_ref))):

            @pl.when(at_ref[0] == bit)
            def _():
                for i in range(pairs):
                    zero[r, i] = whole[2 * i * rows : (2 * i + 1) * rows, half:]
                    one[r, i] = whole[(2 * i + 1) * rows : (2 * i + 2) * rows, half:]


def grads_kernel(keep_w, came_w, keep_m, came_m, qkv_ref, out_ref, mlp_ref, col_ref, row_ref):
    cols = out_ref.shape[1]
    col_ref[...] = jnp.zeros_like(col_ref)
    row_sums = []
    for i, (keep, came) in enumerate(((keep_w, came_w), (keep_m, came_m))):
        total = keep[...].astype(f32) + came[...].astype(f32)
        for j in range(3):
            grad = total[:, j * cols : (j + 1) * cols]
            if i == 0:
                qkv_ref[j] = grad
            elif j == 0:
                out_ref[...] = grad
            else:
                mlp_ref[j - 1] = grad
            square = grad * grad
            col_ref[3 * i + j : 3 * i + j + 1, :] = jnp.sum(square, axis=0, keepdims=True)
            row_sums.append(jnp.sum(square, axis=1, keepdims=True))
    zeros = jnp.zeros((row_sums[0].shape[0], LANES - 6), f32)
    row_ref[...] = jnp.concatenate([*row_sums, zeros], axis=1).T[:8, :]


def update_kernel(sizes, qkv_ref, out_ref, mlp_ref, col_ref, row_ref, cs_ref, rs_ref, cn_ref, rn_ref, up_ref, sq_ref):
    total_cols, width = sizes
    col_new = BETA_TWO * cs_ref[...] + (1.0 - BETA_TWO) * col_ref[:6, :] / width
    row_new = BETA_TWO * rs_ref[...] + (1.0 - BETA_TWO) * row_ref[:6, :] / total_cols
    cn_ref[...] = col_new
    rn_ref[...] = row_new
    rows = row_new.shape[1]
    row_cols = jnp.concatenate([row_new, jnp.ones((2, rows), f32)], axis=0).T
    sq_ref[...] = jnp.zeros_like(sq_ref)
    for i in range(6):
        grad = qkv_ref[i] if i < 3 else out_ref[...] if i == 3 else mlp_ref[i - 4]
        update = grad * lax.rsqrt(row_cols[:, i : i + 1] * col_new[i : i + 1, :])
        up_ref[i] = update
        sq_ref[i : i + 1, :] = jnp.sum(update * update, axis=0, keepdims=True)


def step_kernel(up_ref, step_ref, qkv_ref, out_ref, mlp_ref, qkv_new, out_new, mlp_new):
    for i in range(6):
        old, new = (qkv_ref, qkv_new) if i < 3 else (mlp_ref, mlp_new)
        change = step_ref[i : i + 1, :] * up_ref[i]
        if i == 3:
            out_new[...] = out_ref[...] - change
        else:
            new[i % 4] = old[i % 4] - change


def shards(
    tokens,
    cotangent,
    lengths,
    qkv,
    out_proj,
    mlp,
    gains,
    query_scale,
    row_second,
    col_second,
    gain_second,
    scale_second,
):
    n_tensor, n_seq = lax.axis_size("tensor"), lax.axis_size("seq")
    seq_index, ten_index = lax.axis_index("seq"), lax.axis_index("tensor")
    tok_dev, width = tokens.shape
    share = cotangent.shape[0]
    rows_own, cols_own = qkv.shape[1], qkv.shape[2]
    heads = cols_own // HD
    row_first = ten_index * share
    flips = list(range(n_tensor))
    sds = jax.ShapeDtypeStruct

    x_share = lax.dynamic_slice_in_dim(tokens, row_first, share, 0)

    padded = -(-3 * cols_own // 256) * 256
    fill = jnp.zeros((rows_own, padded - 3 * cols_own), f32)
    shard_m = jnp.concatenate([out_proj, mlp[0], mlp[1], fill], axis=1).astype(bf16)
    shard_qkv = jnp.concatenate([qkv[0], qkv[1], qkv[2], fill], axis=1).astype(bf16)
    near, far, flips_q = gather_groups(shard_qkv)
    rim_own = lax.ppermute(x_share, "seq", [(i, i + 1) for i in range(n_seq - 1)])
    rims = [rim_own] + [hop(rim_own, "tensor", f) for f in flips[2::2]]
    flips_rim = flips[::2] + flips[1::2]
    rims = rims + [hop(piece, "tensor", 1) for piece in rims]
    across = {f: {} for f in flips[2::2]}

    def send_across(g, pairs, *earlier):
        for f in across:
            across[f][g] = hop(after(pairs[g], *earlier), "tensor", f)
        return [across[f][g] for f in across]

    def second(f, pairs):
        if not f:
            send_across(0, pairs)
            return near[-1], far[1]
        return send_across(f, pairs, rims[: n_tensor // 2])

    pairs_m = gather_pairs(shard_m, (near[1], far[0]), second)
    for g in pairs_m:
        if g % 2:
            send_across(g, pairs_m, list(across[flips[2]].values())[-1])
    flips_m = list(pairs_m)
    mats = {0: [jnp.stack([pairs_m[g] for g in flips_m])]}
    mats[1] = [hop(mats[0][0], "tensor", 1)]
    for f in across:
        mats[f] = [across[f][g][None] for g in flips_m]
    low, outer = seq_index % 2, seq_index // 2
    spots_share = [(ten_index ^ f) * share for f in flips]
    spots_q = [(outer ^ f) * 2 * rows_own for f in flips_q]
    spots_rim = [(ten_index ^ f) * share for f in flips_rim]
    spots_m = [(outer ^ f) * 2 * rows_own for f in flips_m]

    places = seq_index * tok_dev + jnp.arange(tok_dev, dtype=jnp.int32)
    ends = jnp.cumsum(lengths[0])
    passed = ends[None, :] <= places[:, None]
    doc_start = jnp.max(jnp.where(passed, ends[None, :], 0), axis=1)
    lo = jnp.maximum(places - (WINDOW - 1), doc_start)
    lo = jnp.where(places >= ends[-1], places, lo)
    lo = (lo - (seq_index * tok_dev - WINDOW)).astype(jnp.int32)[None, :]

    factor = jax.nn.softplus(query_scale) * SCALE_ROOT
    scale_cols = jnp.tile(factor, heads)[None, :]
    table = WINDOW + tok_dev
    pair_flops = tok_dev * SPAN * cols_own * 2
    h_all, queries, key_rows, value_rows, context, log_totals, w_qkv = vmem_call(
        functools.partial(attend_kernel, heads, (len(near), len(rims))),
        (
            sds((table, width), bf16),
            sds((tok_dev, cols_own), bf16),
            sds((table, cols_own), bf16),
            sds((table, cols_own), bf16),
            sds((tok_dev, cols_own), bf16),
            sds((heads, tok_dev), f32),
            sds((width, padded), bf16),
        ),
        [
            pltpu.VMEM((heads, table, LANES), bf16),
            pltpu.VMEM((cols_own, table), bf16),
            pltpu.VMEM((SPAN, BLOCK), f32),
        ],
        2 * table * width * 3 * cols_own + 6 * pair_flops,
        44,
        jnp.stack([low, *spots_q, *spots_rim]),
        tokens,
        *rims,
        *near,
        *far,
        gains[:1],
        scale_cols,
        lo,
    )

    for f in flips[2::2]:
        mats[f + 1] = [hop(after(piece, context), "tensor", 1) for piece in mats[f]]

    def share_of(values, f):
        return lax.dynamic_slice_in_dim(values, (ten_index ^ f) * share, share, 0)

    ctx = [share_of(context, f) for f in flips]
    ctx = [ctx[0]] + [hop(ctx[f], "tensor", f) for f in flips[1:]]
    shape_share = (share, width)
    outs = vmem_call(
        functools.partial(share_kernel, [len(mats[f]) for f in flips]),
        (
            sds(shape_share, f32),
            sds(shape_share, f32),
            sds((1, width), f32),
            sds((2, share, width), bf16),
            sds((2, share, n_tensor // 2 * cols_own), bf16),
            sds((2, share, n_tensor // 2 * cols_own), bf16),
            *[sds((share, cols_own), bf16) for _ in flips],
        ),
        [pltpu.VMEM((width, width), bf16) for _ in range(3)],
        2 * 6 * share * width * width,
        44,
        jnp.stack(spots_m),
        *ctx,
        *[piece for f in flips for piece in mats[f]],
        x_share,
        cotangent,
        gains[1:],
    )
    result, grad_mid, gain_two_grad, rows_two, even, odd = outs[:6]
    gctx = outs[6:]
    gctx = [gctx[0]] + [hop(gctx[f], "tensor", f) for f in flips[1:]]

    n_even, half = n_tensor // 2, padded // 2
    halves = sds((n_even, n_seq // 4, 2 * rows_own, half), bf16)
    *firsts, send, keep = vmem_call(
        functools.partial(share_grads_kernel, n_even),
        (*[sds((width, half), bf16) for _ in range(n_even)], halves, halves),
        [],
        2 * 3 * share * width * width,
        44,
        (outer % 2)[None],
        *ctx[::2],
        hop(jnp.concatenate(ctx[1::2], axis=1), "tensor", 1),
        rows_two,
        hop(rows_two, "tensor", 1),
        even,
        hop(odd, "tensor", 1),
        cotangent,
        hop(cotangent, "tensor", 1),
    )
    came = [hop(part, "tensor", 2 * i) for i, part in enumerate(firsts) if i]
    turned = hop(send, "seq", 2)
    log_totals, _ = lax.optimization_barrier((log_totals, firsts + [send]))

    grad_q, grad_kv, scale_raw, *grad_w = vmem_call(
        functools.partial(attend_back_kernel, heads, n_tensor),
        (
            sds((tok_dev, cols_own), bf16),
            sds((table, 2 * cols_own), bf16),
            sds((1, cols_own), f32),
            *[sds((n_seq // 2, rows_own, padded), bf16) for _ in range(2)],
        ),
        [
            pltpu.VMEM((heads, table, LANES), bf16),
            pltpu.VMEM((heads, table, LANES), bf16),
            pltpu.VMEM((cols_own, table), bf16),
            pltpu.VMEM((width, table), bf16),
            pltpu.VMEM((tok_dev, cols_own), bf16),
            pltpu.VMEM((heads, table, LANES), f32),
            pltpu.VMEM((heads, table, LANES), f32),
            pltpu.VMEM((SPAN, BLOCK), f32),
        ],
        14 * pair_flops + 2 * table * width * 3 * cols_own,
        56,
        jnp.stack([low, *spots_share]),
        *gctx,
        queries,
        key_rows,
        value_rows,
        scale_cols,
        lo,
        log_totals,
        h_all,
    )
    scale_part = (
        jnp.sum((scale_raw / scale_cols).reshape(heads, HD), axis=0)
        * SCALE_ROOT
        * jax.nn.sigmoid(query_scale)
    )
    bits = n_seq.bit_length() - 1
    part_rows = sds((n_even, share, 2 * width), bf16)
    even_rows, odd_rows = vmem_call(
        functools.partial(rows_kernel, n_tensor),
        (part_rows, part_rows),
        [],
        2 * (tok_dev * 5 * cols_own) * width,
        44,
        jnp.stack(spots_share),
        grad_q,
        grad_kv,
        w_qkv,
    )
    turned_w = hop(grad_w[0], "seq", 1)
    from_core_rows = hop(odd_rows, "tensor", 1)

    first = firsts[0].astype(f32)
    for part in came:
        first = first + part.astype(f32)
    first = first.reshape(*[2] * bits, rows_own, half)
    send, keep_first = scatter_step(first, list(range(bits)), 1)
    second = keep.astype(f32) + turned.astype(f32)
    sends = [second[i].astype(bf16) for i in range(1, n_even)]
    came_first = hop(send, "seq", 2)
    far_second = [hop(part, "tensor", 2 * i + 2) for i, part in enumerate(sends)]
    from_core_rows = after(from_core_rows, far_second)
    sums = [even_rows[i].astype(f32) + from_core_rows[i].astype(f32) for i in range(n_even)]
    sum_sends = [part.astype(bf16) for part in sums[1:]]

    rest = [0, *range(2, bits)]
    first = keep_first + came_first.astype(f32)
    second = second[0]
    for part in far_second:
        second = second + part.astype(f32)
    second = second.reshape(*[2] * (bits - 1), rows_own, half)
    both = jnp.concatenate([first, second], axis=-1)
    far_rim = [hop(part[:, :width], "tensor", 2 * i + 2) for i, part in enumerate(sum_sends)]
    rim_one, grad_one = sums[0][:, :width], sums[0][:, width:]
    for part in far_rim:
        rim_one = rim_one + part.astype(f32)
    far_here = [
        hop(after(part[:, width:], far_rim), "tensor", 2 * i + 2)
        for i, part in enumerate(sum_sends)
    ]
    for part in far_here:
        grad_one = grad_one + part.astype(f32)
    high = list(range(1, bits))
    own_qkv = grad_w[1].astype(f32) + after(turned_w, sum_sends, came_first).astype(f32)
    own_qkv = own_qkv.reshape(*[2] * (bits - 1), *own_qkv.shape[1:])
    keep_m, came_m = scatter_seq(both, rest, rest[::-1])
    keep_w, came_w = scatter_seq(own_qkv, high, high, far_rim)
    back = lax.ppermute(rim_one.astype(bf16), "seq", [(i, i - 1) for i in range(1, n_seq)])
    grad_one = grad_one + back.astype(f32)
    came_w = after(came_w, back)
    x_part = x_share.astype(f32)
    factor_one = lax.rsqrt(jnp.mean(x_part * x_part, axis=-1, keepdims=True) + EPSILON)
    norm_one = x_part * factor_one
    gain_one_grad = jnp.sum(grad_one * norm_one, axis=0)
    scaled = grad_one * gains[0]
    tokens_grad = grad_mid + factor_one * (
        scaled - norm_one * jnp.mean(scaled * norm_one, axis=-1, keepdims=True)
    )

    total_cols = cols_own * n_tensor
    shape_w = (sds((3, rows_own, cols_own), f32), sds((rows_own, cols_own), f32))
    shape_w = (*shape_w, sds((2, rows_own, cols_own), f32))
    *grads, col_part, row_part = vmem_call(
        grads_kernel,
        (*shape_w, sds((8, cols_own), f32), sds((8, rows_own), f32)),
        [],
        1e9,
        32,
        keep_w,
        came_w,
        keep_m,
        came_m,
    )
    col_new, row_new, unscaled, unscaled_part = vmem_call(
        functools.partial(update_kernel, (total_cols, width)),
        (
            sds((6, cols_own), f32),
            sds((6, rows_own), f32),
            sds((6, rows_own, cols_own), f32),
            sds((6, cols_own), f32),
        ),
        [],
        1e9,
        32,
        *grads,
        summed(col_part, "seq"),
        summed(row_part, "tensor"),
        col_second,
        row_second,
    )

    gain_part = jnp.stack([gain_one_grad, gain_two_grad[0]])
    gain_part = gain_part.reshape(2, n_seq, rows_own).transpose(1, 0, 2).reshape(n_seq, 2 * rows_own)
    rest = jnp.concatenate(
        [
            scale_part,
            jnp.sum(unscaled_part, axis=1),
            jnp.sum(row_part[:6], axis=1),
            jnp.sum(row_second, axis=1) / n_tensor,
        ]
    )
    rest = jnp.broadcast_to(rest, (n_seq, HD + 18))
    last = jnp.concatenate([gain_part, rest], axis=1)
    size = -(-last.shape[1] // 1024) * 1024
    last = jnp.pad(last, ((0, 0), (0, size - last.shape[1]))).reshape(n_seq, 1, size // 128, 128)
    last = jnp.broadcast_to(last, (n_seq, n_tensor, size // 128, 128))
    last = last.reshape(n_seq * n_tensor, size // 128, 128)
    got = lax.all_to_all(last, ("seq", "tensor"), split_axis=0, concat_axis=0)
    gains_grad, scale_grad, unscaled_square, all_square, old_sums = unpacked(
        jnp.sum(got, axis=0), (2, rows_own), (HD,), (6,), (6,), (6,)
    )
    row_mean = (BETA_TWO * old_sums + (1.0 - BETA_TWO) * all_square / total_cols) / width
    update_rms = jnp.sqrt(row_mean * unscaled_square / (width * total_cols))
    step = STEP_RATE * jnp.sqrt(row_mean) / jnp.maximum(1.0, update_rms / CLIP_LEVEL)
    fresh = vmem_call(
        step_kernel,
        shape_w,
        [],
        1e9,
        32,
        unscaled,
        jnp.broadcast_to(step[:, None], (6, cols_own)),
        qkv,
        out_proj,
        mlp,
    )
    gains_own = lax.dynamic_slice_in_dim(gains, seq_index * rows_own, rows_own, 1)
    gain_second_new = BETA_TWO * gain_second + (1.0 - BETA_TWO) * gains_grad * gains_grad
    gains_new = gains_own - VECTOR_RATE * gains_grad * lax.rsqrt(gain_second_new)
    scale_second_new = BETA_TWO * scale_second + (1.0 - BETA_TWO) * scale_grad * scale_grad
    scale_new = query_scale - VECTOR_RATE * scale_grad * lax.rsqrt(scale_second_new)
    return (
        result,
        tokens_grad,
        *grads,
        gains_grad,
        scale_grad,
        *fresh,
        gains_new,
        scale_new,
        row_new,
        col_new,
        update_rms,
        gain_second_new,
        scale_second_new,
    )


def solution(mesh):
    return jax.shard_map(
        shards,
        mesh=mesh,
        in_specs=(
            P("seq", None),
            P(("seq", "tensor"), None),
            P(),
            P(None, "seq", "tensor"),
            P("seq", "tensor"),
            P(None, "seq", "tensor"),
            P(),
            P(),
            P(None, "seq"),
            P(None, "tensor"),
            P(None, "seq"),
            P(),
        ),
        out_specs=(
            P(("seq", "tensor"), None),
            P(("seq", "tensor"), None),
            P(None, "seq", "tensor"),
            P("seq", "tensor"),
            P(None, "seq", "tensor"),
            P(None, "seq"),
            P(),
            P(None, "seq", "tensor"),
            P("seq", "tensor"),
            P(None, "seq", "tensor"),
            P(None, "seq"),
            P(),
            P(None, "seq"),
            P(None, "tensor"),
            P(),
            P(None, "seq"),
            P(),
        ),
        check_vma=False,
    )
```

```python
import functools
import math

import jax
import jax.numpy as jnp
from jax import lax
from jax.experimental import pallas as pl
from jax.experimental.pallas import tpu as pltpu
from jax.sharding import PartitionSpec as P

HD = 80
WINDOW = 1024
BLOCK = 256
SPAN = WINDOW + BLOCK
LANES = 128

EPSILON = 1e-06
LOG_BASE = 1.442695
BETA_TWO = 0.5
STEP_RATE = 0.3
CLIP_LEVEL = 0.1
VECTOR_RATE = 0.3
NEGATIVE = -1e30
SCALE_ROOT = LOG_BASE / math.sqrt(HD)
MIB = 1024 * 1024

bf16 = jnp.bfloat16
f32 = jnp.float32


def dot(left, right, dims):
    return lax.dot_general(left, right, (dims, ((), ())), preferred_element_type=f32)


def vmem_call(body, outs, scratch, flops, limit, *args, far_in=(), far_out=()):
    size = sum(math.prod(a.shape) * a.dtype.itemsize for a in (*args, *outs))
    space = pl.BlockSpec(memory_space=pltpu.VMEM)
    scalars = pl.BlockSpec(memory_space=pltpu.SMEM)
    anywhere = pl.BlockSpec(memory_space=pl.ANY)
    return pl.pallas_call(
        body,
        out_shape=outs,
        in_specs=[
            scalars if a.ndim == 1 else anywhere if i in far_in else space
            for i, a in enumerate(args)
        ],
        out_specs=[anywhere if i in far_out else space for i in range(len(outs))],
        scratch_shapes=scratch,
        compiler_params=pltpu.CompilerParams(vmem_limit_bytes=limit * MIB),
        cost_estimate=pl.CostEstimate(flops=8 * int(flops), bytes_accessed=size, transcendentals=0),
    )(*args)


def hop(value, axis, flip):
    peers = lax.axis_size(axis)
    return lax.ppermute(value, axis, [(i, i ^ flip) for i in range(peers)])


def after(value, *earlier):
    return lax.optimization_barrier((value, *earlier))[0]


def put(table, piece, row):
    return lax.dynamic_update_slice_in_dim(table, piece, row, 0)


def pair_up(piece):
    other = hop(piece, "seq", 1)
    low = lax.axis_index("seq") % 2 == 0
    return jnp.concatenate([jnp.where(low, piece, other), jnp.where(low, other, piece)], axis=0)


def gather_pairs(shard, first, second):
    peers = lax.axis_size("seq")
    pairs = {}
    for f in range(0, peers // 2, 2):
        pairs[f] = pair_up(after(hop(after(shard, first), "seq", 2 * f), first) if f else shard)
    for f in range(0, peers // 2, 2):
        pairs[f + 1] = hop(after(pairs[f], second(f, pairs)), "seq", 2)
    return pairs


def gather_groups(shard):
    peers = lax.axis_size("seq")
    evens = list(range(0, peers // 2, 2))
    groups = [shard[None]]
    if evens[1:]:
        groups.append(jnp.stack([hop(shard, "seq", 2 * f) for f in evens[1:]]))
    others = [hop(group, "seq", 1) for group in groups]
    groups.append(hop(jnp.concatenate(groups, axis=0), "seq", 2))
    others.append(hop(groups[-1], "seq", 1))
    return groups, others, evens + [f + 1 for f in evens]


def scatter_step(total, left, k):
    at = len(left) - 1 - left.index(k)
    bit = (lax.axis_index("seq") >> k) & 1
    send = lax.dynamic_index_in_dim(total, 1 - bit, at, keepdims=False).astype(bf16)
    return send, lax.dynamic_index_in_dim(total, bit, at, keepdims=False)


def scatter_seq(total, left, order, *earlier):
    left = list(left)
    for k in order:
        send, keep = scatter_step(total, left, k)
        send = after(send, *earlier) if len(left) == 1 else send
        left.remove(k)
        came = hop(send, "seq", 1 << k)
        if left:
            total = keep.astype(f32) + came.astype(f32)
    return keep, came


def summed(value, axis):
    flip = 1
    while flip < lax.axis_size(axis):
        value = value + hop(value, axis, flip)
        flip *= 2
    return value


def packed(*values):
    flat = jnp.concatenate([v.reshape(-1) for v in values])
    size = -(-flat.shape[0] // 1024) * 1024
    return jnp.pad(flat, (0, size - flat.shape[0])).reshape(size // 128, 128)


def unpacked(table, *shapes):
    flat, out, at = table.reshape(-1), [], 0
    for shape in shapes:
        size = math.prod(shape)
        out.append(flat[at : at + size].reshape(shape))
        at += size
    return out


def head_of(rows, h):
    zeros = jnp.zeros((rows.shape[0], LANES - HD), rows.dtype)
    return jnp.concatenate([rows[:, h * HD : (h + 1) * HD], zeros], axis=1)


def attend_kernel(heads, counts, *refs):
    n_near, n_rim, n_parts = counts
    refs = list(refs)

    def take(n):
        out = refs[:n]
        del refs[:n]
        return out

    at_ref, tok_in = take(2)
    rims, near, far = take(n_rim), take(n_near), take(n_near)
    gain_ref, sc_ref, lo_ref = take(3)
    h_out, q_out, k_out, v_out, w_out, lse_ref = take(6)
    pieces = take(n_parts)
    x_ref, h_ref, w_ref, q_ref, k_ref, v_ref, kh, vt, bias, c_ref = take(10)
    stages, (in_sem, out_sem) = take(2 * n_near), take(2)
    cols = heads * HD
    rows = q_ref.shape[0]

    arrive = []

    def bring(source, target):
        arrive.append(pltpu.make_async_copy(source, target, in_sem.at[len(arrive)]))
        arrive[-1].start()
        return arrive[-1]

    weights = [bring(a, b) for a, b in zip((*near, *far), stages)]
    own = bring(tok_in, x_ref.at[pl.ds(WINDOW, rows), :])
    spot = 1 + sum(a.shape[0] for a in near)
    rim_copies = []
    for i, rim in enumerate(rims):
        place = pl.multiple_of(at_ref[spot + i], 16)
        rim_copies.append(bring(rim, x_ref.at[pl.ds(place, rim.shape[0]), :]))
    spot += n_rim

    leave = []

    def send(source, target):
        leave.append(pltpu.make_async_copy(source, target, out_sem.at[len(leave)]))
        leave[-1].start()

    for copy in weights:
        copy.wait()
    turn = 1
    for one, two in zip(stages[:n_near], stages[n_near:]):
        for i in range(one.shape[0]):
            at = pl.ds(pl.multiple_of(at_ref[turn], 16), 2 * one.shape[1])
            turn += 1

            @pl.when(at_ref[0] == 0)
            def _():
                w_ref[at, :] = jnp.concatenate([one[i], two[i]], axis=0)

            @pl.when(at_ref[0] == 1)
            def _():
                w_ref[at, :] = jnp.concatenate([two[i], one[i]], axis=0)

    send(w_ref, w_out)

    blocks = h_ref.shape[0] // BLOCK
    own.wait()
    for j in range(blocks):
        i = (j + WINDOW // BLOCK) % blocks
        if i == 0:
            for copy in rim_copies:
                copy.wait()
        at = slice(i * BLOCK, (i + 1) * BLOCK)
        values = x_ref[at, :].astype(f32)
        factor = lax.rsqrt(jnp.mean(values * values, axis=-1, keepdims=True) + EPSILON)
        normed = (values * factor * gain_ref[...]).astype(bf16)
        h_ref[at, :] = normed
        proj = dot(normed, w_ref[:, : 3 * cols], ((1,), (0,)))
        if i * BLOCK >= WINDOW:
            q_ref[i * BLOCK - WINDOW : (i + 1) * BLOCK - WINDOW, :] = (
                proj[:, :cols] * sc_ref[...]
            ).astype(bf16)
        k_rows = proj[:, cols : 2 * cols].astype(bf16)
        v_rows = proj[:, 2 * cols :].astype(bf16)
        k_ref[at, :] = k_rows
        v_ref[at, :] = v_rows
        vt[:, at] = v_rows.T
        for h in range(heads):
            kh[h, at, :] = head_of(k_rows, h)
    for source, target in ((h_ref, h_out), (q_ref, q_out), (k_ref, k_out), (v_ref, v_out)):
        send(source, target)

    steps = [(b, h) for b in range(rows // BLOCK) for h in range(heads)]

    def begin(b, h):
        if h == 0:
            fill_bias(bias, b, lo_ref)
        keys = slice(b * BLOCK, b * BLOCK + SPAN)
        q_head = head_of(q_ref[b * BLOCK : (b + 1) * BLOCK, :], h)
        return dot(kh[h, keys, :], q_head, ((1,), (1,))) + bias[b % 2]

    ready, mixed = begin(*steps[0]), []
    for i, (b, h) in enumerate(steps):
        s = ready
        if i + 1 < len(steps):
            ready = begin(*steps[i + 1])
        at, keys = slice(b * BLOCK, (b + 1) * BLOCK), slice(b * BLOCK, b * BLOCK + SPAN)
        top = jnp.max(s, axis=0, keepdims=True)
        p = jnp.exp(s - top)
        total = jnp.sum(p, axis=0, keepdims=True)
        part = dot(vt[h * HD : (h + 1) * HD, keys], p.astype(bf16), ((1,), (0,)))
        mixed.append((part / total).T)
        lse_ref[h : h + 1, at] = top + jnp.log(total)
        if h == heads - 1:
            c_ref[at, :] = jnp.concatenate(mixed, axis=1).astype(bf16)
            mixed = []
    for i, piece in enumerate(pieces):
        share = piece.shape[0]
        piece[...] = c_ref[pl.ds(pl.multiple_of(at_ref[spot + i], 16), share), :]
    for copy in leave:
        copy.wait()


def fill_bias(bias, b, lo_ref):
    k_place = b * BLOCK + lax.broadcasted_iota(jnp.int32, (SPAN, BLOCK), 0)
    q_place = b * BLOCK + WINDOW + lax.broadcasted_iota(jnp.int32, (SPAN, BLOCK), 1)
    seen = (k_place >= lo_ref[:, b * BLOCK : (b + 1) * BLOCK]) & (k_place <= q_place)
    bias[b % 2] = jnp.where(seen, 0.0, NEGATIVE)


def attend_back_kernel(heads, n_parts, at_ref, *refs):
    parts = refs[:n_parts]
    q_ref, k_ref, v_ref, sc_ref, lo_ref, lse_ref, h_ref = refs[n_parts : n_parts + 7]
    outs = refs[n_parts + 7 :]
    dq_ref, dkv_ref, part_ref = outs[:3]
    send_ref, keep_ref = outs[3:5]
    kh, vh, kt, ht, g_ref, dk, dv, bias, h_rows, sem = outs[5:]
    arrive = pltpu.make_async_copy(h_ref, h_rows, sem)
    arrive.start()
    rows, cols = q_ref.shape
    for i, part in enumerate(parts):
        share = part.shape[0]
        g_ref[pl.ds(pl.multiple_of(at_ref[1 + i], 16), share), :] = part[...]
    kt[...] = k_ref[...].T
    for h in range(heads):
        kh[h] = head_of(k_ref[...], h)
        vh[h] = head_of(v_ref[...], h)
    part_ref[...] = jnp.zeros_like(part_ref)

    steps = [(b, h) for b in range(rows // BLOCK) for h in range(heads)]

    def begin(b, h):
        if h == 0:
            fill_bias(bias, b, lo_ref)
        at, keys = slice(b * BLOCK, (b + 1) * BLOCK), slice(b * BLOCK, b * BLOCK + SPAN)
        q_head, g_head = head_of(q_ref[at, :], h), head_of(g_ref[at, :], h)
        s = dot(kh[h, keys, :], q_head, ((1,), (1,))) + bias[b % 2]
        return s, dot(vh[h, keys, :], g_head, ((1,), (1,))), q_head, g_head

    ready, grads = begin(*steps[0]), []
    for i, (b, h) in enumerate(steps):
        s, dp, q_head, g_head = ready
        if i + 1 < len(steps):
            ready = begin(*steps[i + 1])
        at, keys = slice(b * BLOCK, (b + 1) * BLOCK), slice(b * BLOCK, b * BLOCK + SPAN)
        p = jnp.exp(s - lse_ref[h : h + 1, at])
        inner = jnp.sum(p * dp, axis=0, keepdims=True)
        ds = (p * (dp - inner)).astype(bf16)
        g_value, g_key = dot(p.astype(bf16), g_head, ((1,), (0,))), dot(ds, q_head, ((1,), (0,)))
        for table, part in ((dv, g_value), (dk, g_key)):
            if b:
                table[h, b * BLOCK : b * BLOCK + WINDOW, :] += part[:WINDOW]
                table[h, b * BLOCK + WINDOW : b * BLOCK + SPAN, :] = part[WINDOW:]
            else:
                table[h, keys, :] = part
        grads.append(dot(kt[h * HD : (h + 1) * HD, keys], ds, ((1,), (0,))).T)
        if h == heads - 1:
            grad, grads = jnp.concatenate(grads, axis=1), []
            part_ref[...] += jnp.sum(grad * q_ref[at, :].astype(f32), axis=0, keepdims=True)
            dq_ref[at, :] = (grad * sc_ref[...]).astype(bf16)
    arrive.wait()
    for i in range(k_ref.shape[0] // BLOCK):
        at = pl.ds(i * BLOCK, BLOCK)
        both = [table[h, at, :HD] for table in (dk, dv) for h in range(heads)]
        dkv_ref[at, :] = jnp.concatenate(both, axis=1).astype(bf16)
        ht[:, at] = h_rows[at, :].T
    gw_q = dot(ht[:, WINDOW:], dq_ref[...], ((1,), (0,))).astype(bf16)
    gw_kv = dot(ht[...], dkv_ref[...], ((1,), (0,))).astype(bf16)
    outer, own, padded = send_ref.shape
    zeros = jnp.zeros((2 * outer * own, padded - 3 * cols), bf16)
    whole = jnp.concatenate([gw_q, gw_kv, zeros], axis=1)
    for low in range(2):

        @pl.when(at_ref[0] == low)
        def _():
            for i in range(2 * outer):
                to = keep_ref if i % 2 == low else send_ref
                to[i // 2] = whole[i * own : (i + 1) * own]


def rows_kernel(parts, at_ref, q_ref, kv_ref, w_ref, even_ref, odd_ref):
    cols, width = q_ref.shape[1], w_ref.shape[0]
    share = even_ref.shape[1]
    for f in range(parts):
        at = pl.multiple_of(at_ref[f], 16)
        here = pl.ds(pl.multiple_of(at + WINDOW, 16), share)
        to = odd_ref if f % 2 else even_ref
        grads = jnp.concatenate([q_ref[pl.ds(at, share), :], kv_ref[here, :]], axis=1)
        to[f // 2, :, width:] = dot(grads, w_ref[:, : 3 * cols], ((1,), (1,))).astype(bf16)
        to[f // 2, :, :width] = dot(
            kv_ref[pl.ds(at, share), :], w_ref[:, cols : 3 * cols], ((1,), (1,))
        ).astype(bf16)


def rows_kernel(parts, at_ref, q_ref, kv_ref, w_ref, even_ref, odd_ref):
    cols, width = q_ref.shape[1], w_ref.shape[0]
    share = even_ref.shape[1]
    for f in range(parts):
        at = pl.multiple_of(at_ref[f], 16)
        here = pl.ds(pl.multiple_of(at + WINDOW, 16), share)
        to = odd_ref if f % 2 else even_ref
        grads = jnp.concatenate([q_ref[pl.ds(at, share), :], kv_ref[here, :]], axis=1)
        to[f // 2, :, width:] = dot(grads, w_ref[:, : 3 * cols], ((1,), (1,))).astype(bf16)
        to[f // 2, :, :width] = dot(
            kv_ref[pl.ds(at, share), :], w_ref[:, cols : 3 * cols], ((1,), (1,))
        ).astype(bf16)


def share_kernel(counts, at_ref, *refs):
    peers = len(counts)
    ctx, refs = refs[:peers], refs[peers:]
    mats = [refs[sum(counts[:r]) : sum(counts[: r + 1])] for r in range(peers)]
    refs = refs[sum(counts) :]
    x_ref, cot_ref, gain_ref = refs[:3]
    outs = refs[3:]
    res_ref, gmid_ref, part_ref, rows_ref, even_ref, odd_ref = outs[:6]
    gctx = outs[6 : 6 + peers]
    w_out, w_in, w_back = outs[6 + peers :]
    cols = ctx[0].shape[1]
    for r, pieces in enumerate(mats):
        for i, (m, k) in enumerate((m, k) for m in pieces for k in range(m.shape[0])):
            at = pl.ds(pl.multiple_of(at_ref[i], 16), m.shape[1])
            for j, w in enumerate((w_out, w_in, w_back)):
                w[at, r * cols : (r + 1) * cols] = m[k, :, j * cols : (j + 1) * cols]
    gain = gain_ref[...]
    mixed = jnp.concatenate([c[...] for c in ctx], axis=1)
    mid = x_ref[...].astype(f32) + dot(mixed, w_out[...], ((1,), (1,)))
    factor = lax.rsqrt(jnp.mean(mid * mid, axis=-1, keepdims=True) + EPSILON)
    normed = mid * factor
    h2 = (normed * gain).astype(bf16)
    rows_ref[1] = h2
    cot = cot_ref[...]
    pre = dot(h2, w_in[...], ((1,), (0,)))
    g_hid = dot(cot, w_back[...], ((1,), (0,)))
    sig = 1.0 / (1.0 + jnp.exp(-pre))
    hidden = (pre * sig).astype(bf16)
    g_pre = (g_hid * sig * (1.0 + pre * (1.0 - sig))).astype(bf16)
    for r in range(peers):
        half, to = odd_ref if r % 2 else even_ref, slice(r // 2 * cols, (r // 2 + 1) * cols)
        half[0, :, to] = g_pre[:, r * cols : (r + 1) * cols]
        half[1, :, to] = hidden[:, r * cols : (r + 1) * cols]
    res_ref[...] = mid + dot(hidden, w_back[...], ((1,), (1,)))
    g_h2 = dot(g_pre, w_in[...], ((1,), (1,)))
    part_ref[...] = jnp.sum(g_h2 * normed, axis=0, keepdims=True)
    scaled = g_h2 * gain
    back = factor * (scaled - normed * jnp.mean(scaled * normed, axis=-1, keepdims=True))
    g_mid = cot.astype(f32) + back
    gmid_ref[...] = g_mid
    gm = g_mid.astype(bf16)
    rows_ref[0] = gm
    g_mixed = dot(gm, w_out[...], ((1,), (0,))).astype(bf16)
    for r, out in enumerate(gctx):
        out[...] = g_mixed[:, r * cols : (r + 1) * cols]


def share_grads_kernel(count, at_ref, *refs):
    ctx, ctx_far = refs[:count], refs[count]
    rows_ref, rows_far, even_ref, odd_far, cot_ref, cot_far = refs[count + 1 : count + 7]
    firsts, send_ref, keep_ref = refs[count + 7 : 2 * count + 7], *refs[2 * count + 7 :]
    lefts = [
        jnp.concatenate([one.T, two.T], axis=1)
        for one, two in (
            (rows_ref[0], rows_far[0]),
            (rows_ref[1], rows_far[1]),
            (cot_ref[...], cot_far[...]),
        )
    ]
    half, cols = firsts[0].shape[-1], ctx[0].shape[1]
    zeros = jnp.zeros((firsts[0].shape[0], 2 * half - 3 * cols), bf16)
    pairs, rows = send_ref.shape[1:3]
    for r in range(count):
        to = slice(r * cols, (r + 1) * cols)
        rights = (
            (ctx[r][...], ctx_far[:, to]),
            (even_ref[0, :, to], odd_far[0, :, to]),
            (even_ref[1, :, to], odd_far[1, :, to]),
        )
        parts = [
            dot(left, jnp.concatenate(right, axis=0), ((1,), (0,))).astype(bf16)
            for left, right in zip(lefts, rights)
        ]
        whole = jnp.concatenate([*parts, zeros], axis=1)
        firsts[r][...] = whole[:, :half]
        for bit, (zero, one) in enumerate(((keep_ref, send_ref), (send_ref, keep_ref))):

            @pl.when(at_ref[0] == bit)
            def _():
                for i in range(pairs):
                    zero[r, i] = whole[2 * i * rows : (2 * i + 1) * rows, half:]
                    one[r, i] = whole[(2 * i + 1) * rows : (2 * i + 2) * rows, half:]


def grads_kernel(keep_w, came_w, keep_m, came_m, qkv_ref, out_ref, mlp_ref, col_ref, row_ref):
    cols = out_ref.shape[1]
    col_ref[...] = jnp.zeros_like(col_ref)
    row_sums = []
    for i, (keep, came) in enumerate(((keep_w, came_w), (keep_m, came_m))):
        total = keep[...].astype(f32) + came[...].astype(f32)
        for j in range(3):
            grad = total[:, j * cols : (j + 1) * cols]
            if i == 0:
                qkv_ref[j] = grad
            elif j == 0:
                out_ref[...] = grad
            else:
                mlp_ref[j - 1] = grad
            square = grad * grad
            col_ref[3 * i + j : 3 * i + j + 1, :] = jnp.sum(square, axis=0, keepdims=True)
            row_sums.append(jnp.sum(square, axis=1, keepdims=True))
    zeros = jnp.zeros((row_sums[0].shape[0], LANES - 6), f32)
    row_ref[...] = jnp.concatenate([*row_sums, zeros], axis=1).T[:8, :]


def update_kernel(sizes, qkv_ref, out_ref, mlp_ref, col_ref, row_ref, cs_ref, rs_ref, cn_ref, rn_ref, up_ref, sq_ref):
    total_cols, width = sizes
    col_new = BETA_TWO * cs_ref[...] + (1.0 - BETA_TWO) * col_ref[:6, :] / width
    row_new = BETA_TWO * rs_ref[...] + (1.0 - BETA_TWO) * row_ref[:6, :] / total_cols
    cn_ref[...] = col_new
    rn_ref[...] = row_new
    rows = row_new.shape[1]
    row_cols = jnp.concatenate([row_new, jnp.ones((2, rows), f32)], axis=0).T
    sq_ref[...] = jnp.zeros_like(sq_ref)
    for i in range(6):
        grad = qkv_ref[i] if i < 3 else out_ref[...] if i == 3 else mlp_ref[i - 4]
        update = grad * lax.rsqrt(row_cols[:, i : i + 1] * col_new[i : i + 1, :])
        up_ref[i] = update
        sq_ref[i : i + 1, :] = jnp.sum(update * update, axis=0, keepdims=True)


def step_kernel(up_ref, step_ref, qkv_ref, out_ref, mlp_ref, qkv_new, out_new, mlp_new):
    for i in range(6):
        old, new = (qkv_ref, qkv_new) if i < 3 else (mlp_ref, mlp_new)
        change = step_ref[i : i + 1, :] * up_ref[i]
        if i == 3:
            out_new[...] = out_ref[...] - change
        else:
            new[i % 4] = old[i % 4] - change


def shards(
    tokens,
    cotangent,
    lengths,
    qkv,
    out_proj,
    mlp,
    gains,
    query_scale,
    row_second,
    col_second,
    gain_second,
    scale_second,
):
    n_tensor, n_seq = lax.axis_size("tensor"), lax.axis_size("seq")
    seq_index, ten_index = lax.axis_index("seq"), lax.axis_index("tensor")
    tok_dev, width = tokens.shape
    share = cotangent.shape[0]
    rows_own, cols_own = qkv.shape[1], qkv.shape[2]
    heads = cols_own // HD
    row_first = ten_index * share
    flips = list(range(n_tensor))
    sds = jax.ShapeDtypeStruct

    x_share = lax.dynamic_slice_in_dim(tokens, row_first, share, 0)

    padded = -(-3 * cols_own // 256) * 256
    fill = jnp.zeros((rows_own, padded - 3 * cols_own), f32)
    shard_m = jnp.concatenate([out_proj, mlp[0], mlp[1], fill], axis=1).astype(bf16)
    shard_qkv = jnp.concatenate([qkv[0], qkv[1], qkv[2], fill], axis=1).astype(bf16)
    near, far, flips_q = gather_groups(shard_qkv)
    rim_own = lax.ppermute(x_share, "seq", [(i, i + 1) for i in range(n_seq - 1)])
    rims = [rim_own] + [hop(rim_own, "tensor", f) for f in flips[2::2]]
    flips_rim = flips[::2] + flips[1::2]
    rims = rims + [hop(piece, "tensor", 1) for piece in rims]
    across = {f: {} for f in flips[2::2]}

    def send_across(g, pairs, *earlier):
        for f in across:
            across[f][g] = hop(after(pairs[g], *earlier), "tensor", f)
        return [across[f][g] for f in across]

    def second(f, pairs):
        if not f:
            send_across(0, pairs)
            return near[-1], far[1]
        return send_across(f, pairs, rims[: n_tensor // 2])

    pairs_m = gather_pairs(shard_m, (near[1], far[0]), second)
    for g in pairs_m:
        if g % 2:
            send_across(g, pairs_m, list(across[flips[2]].values())[-1])
    flips_m = list(pairs_m)
    mats = {0: [jnp.stack([pairs_m[g] for g in flips_m])]}
    mats[1] = [hop(mats[0][0], "tensor", 1)]
    for f in across:
        mats[f] = [across[f][g][None] for g in flips_m]
    low, outer = seq_index % 2, seq_index // 2
    spots_share = [(ten_index ^ f) * share for f in flips]
    spots_q = [(outer ^ f) * 2 * rows_own for f in flips_q]
    spots_rim = [(ten_index ^ f) * share for f in flips_rim]
    spots_m = [(outer ^ f) * 2 * rows_own for f in flips_m]

    places = seq_index * tok_dev + jnp.arange(tok_dev, dtype=jnp.int32)
    ends = jnp.cumsum(lengths[0])
    passed = ends[None, :] <= places[:, None]
    doc_start = jnp.max(jnp.where(passed, ends[None, :], 0), axis=1)
    lo = jnp.maximum(places - (WINDOW - 1), doc_start)
    lo = jnp.where(places >= ends[-1], places, lo)
    lo = (lo - (seq_index * tok_dev - WINDOW)).astype(jnp.int32)[None, :]

    factor = jax.nn.softplus(query_scale) * SCALE_ROOT
    scale_cols = jnp.tile(factor, heads)[None, :]
    table = WINDOW + tok_dev
    pair_flops = tok_dev * SPAN * cols_own * 2
    stages = [pltpu.VMEM(part.shape, bf16) for part in (*near, *far)]
    n_in = len(stages) + 1 + len(rims)
    h_all, queries, key_rows, value_rows, w_qkv, log_totals, *ctx = vmem_call(
        functools.partial(attend_kernel, heads, (len(near), len(rims), n_tensor)),
        (
            sds((table, width), bf16),
            sds((tok_dev, cols_own), bf16),
            sds((table, cols_own), bf16),
            sds((table, cols_own), bf16),
            sds((width, padded), bf16),
            sds((heads, tok_dev), f32),
            *[sds((share, cols_own), bf16) for _ in flips],
        ),
        [
            pltpu.VMEM((table, width), bf16),
            pltpu.VMEM((table, width), bf16),
            pltpu.VMEM((width, padded), bf16),
            pltpu.VMEM((tok_dev, cols_own), bf16),
            pltpu.VMEM((table, cols_own), bf16),
            pltpu.VMEM((table, cols_own), bf16),
            pltpu.VMEM((heads, table, LANES), bf16),
            pltpu.VMEM((cols_own, table), bf16),
            pltpu.VMEM((2, SPAN, BLOCK), f32),
            pltpu.VMEM((tok_dev, cols_own), bf16),
            *stages,
            pltpu.SemaphoreType.DMA((n_in,)),
            pltpu.SemaphoreType.DMA((5,)),
        ],
        2 * table * width * 3 * cols_own + 6 * pair_flops,
        56,
        jnp.stack([low, *spots_q, *spots_rim, *spots_share]),
        tokens,
        *rims,
        *near,
        *far,
        gains[:1],
        scale_cols,
        lo,
        far_in=range(1, 1 + n_in),
        far_out=range(5),
    )
    for f in flips[2::2]:
        mats[f + 1] = [hop(after(piece, log_totals), "tensor", 1) for piece in mats[f]]

    ctx = [ctx[0]] + [hop(ctx[f], "tensor", f) for f in flips[1:]]
    shape_share = (share, width)
    outs = vmem_call(
        functools.partial(share_kernel, [len(mats[f]) for f in flips]),
        (
            sds(shape_share, f32),
            sds(shape_share, f32),
            sds((1, width), f32),
            sds((2, share, width), bf16),
            sds((2, share, n_tensor // 2 * cols_own), bf16),
            sds((2, share, n_tensor // 2 * cols_own), bf16),
            *[sds((share, cols_own), bf16) for _ in flips],
        ),
        [pltpu.VMEM((width, width), bf16) for _ in range(3)],
        2 * 6 * share * width * width,
        44,
        jnp.stack(spots_m),
        *ctx,
        *[piece for f in flips for piece in mats[f]],
        x_share,
        cotangent,
        gains[1:],
    )
    result, grad_mid, gain_two_grad, rows_two, even, odd = outs[:6]
    gctx = outs[6:]
    gctx = [gctx[0]] + [hop(gctx[f], "tensor", f) for f in flips[1:]]

    n_even, half = n_tensor // 2, padded // 2
    halves = sds((n_even, n_seq // 4, 2 * rows_own, half), bf16)
    *firsts, send, keep = vmem_call(
        functools.partial(share_grads_kernel, n_even),
        (*[sds((width, half), bf16) for _ in range(n_even)], halves, halves),
        [],
        2 * 3 * share * width * width,
        44,
        (outer % 2)[None],
        *ctx[::2],
        hop(jnp.concatenate(ctx[1::2], axis=1), "tensor", 1),
        rows_two,
        hop(rows_two, "tensor", 1),
        even,
        hop(odd, "tensor", 1),
        cotangent,
        hop(cotangent, "tensor", 1),
    )
    came = [hop(part, "tensor", 2 * i) for i, part in enumerate(firsts) if i]
    turned = hop(send, "seq", 2)
    log_totals, _ = lax.optimization_barrier((log_totals, firsts + [send]))

    grad_q, grad_kv, scale_raw, *grad_w = vmem_call(
        functools.partial(attend_back_kernel, heads, n_tensor),
        (
            sds((tok_dev, cols_own), bf16),
            sds((table, 2 * cols_own), bf16),
            sds((1, cols_own), f32),
            *[sds((n_seq // 2, rows_own, padded), bf16) for _ in range(2)],
        ),
        [
            pltpu.VMEM((heads, table, LANES), bf16),
            pltpu.VMEM((heads, table, LANES), bf16),
            pltpu.VMEM((cols_own, table), bf16),
            pltpu.VMEM((width, table), bf16),
            pltpu.VMEM((tok_dev, cols_own), bf16),
            pltpu.VMEM((heads, table, LANES), f32),
            pltpu.VMEM((heads, table, LANES), f32),
            pltpu.VMEM((2, SPAN, BLOCK), f32),
            pltpu.VMEM((table, width), bf16),
            pltpu.SemaphoreType.DMA,
        ],
        14 * pair_flops + 2 * table * width * 3 * cols_own,
        56,
        jnp.stack([low, *spots_share]),
        *gctx,
        queries,
        key_rows,
        value_rows,
        scale_cols,
        lo,
        log_totals,
        h_all,
        far_in=[n_tensor + 7],
    )
    scale_part = (
        jnp.sum((scale_raw / scale_cols).reshape(heads, HD), axis=0)
        * SCALE_ROOT
        * jax.nn.sigmoid(query_scale)
    )
    bits = n_seq.bit_length() - 1
    part_rows = sds((n_even, share, 2 * width), bf16)
    even_rows, odd_rows = vmem_call(
        functools.partial(rows_kernel, n_tensor),
        (part_rows, part_rows),
        [],
        2 * (tok_dev * 5 * cols_own) * width,
        44,
        jnp.stack(spots_share),
        grad_q,
        grad_kv,
        w_qkv,
    )
    turned_w = hop(grad_w[0], "seq", 1)

    first = firsts[0].astype(f32)
    for part in came:
        first = first + part.astype(f32)
    first = first.reshape(*[2] * bits, rows_own, half)
    send, keep_first = scatter_step(first, list(range(bits)), 1)
    second = keep.astype(f32) + turned.astype(f32)
    sends = [second[i].astype(bf16) for i in range(1, n_even)]
    came_first = hop(send, "seq", 2)
    far_second = [hop(part, "tensor", 2 * i + 2) for i, part in enumerate(sends)]
    from_core_rows = hop(after(odd_rows, turned_w, came_first, far_second), "tensor", 1)
    sums = [even_rows[i].astype(f32) + from_core_rows[i].astype(f32) for i in range(n_even)]
    sum_sends = [part.astype(bf16) for part in sums[1:]]

    parts_m, rest = [], [0, *range(2, bits)]
    first = keep_first + came_first.astype(f32)
    second = second[0]
    for part in far_second:
        second = second + part.astype(f32)
    second = second.reshape(*[2] * (bits - 1), rows_own, half)
    for part, left, order in (
        (first, rest, rest),
        (second, rest, rest[::-1]),
    ):
        parts_m.append(scatter_seq(part, left, order))
    sum_sends = after(sum_sends, turned_w, far_second)
    far_rim = [hop(part[:, :width], "tensor", 2 * i + 2) for i, part in enumerate(sum_sends)]
    rim_one, grad_one = sums[0][:, :width], sums[0][:, width:]
    for part in far_rim:
        rim_one = rim_one + part.astype(f32)
    far_here = [
        hop(after(part[:, width:], far_rim), "tensor", 2 * i + 2)
        for i, part in enumerate(sum_sends)
    ]
    for part in far_here:
        grad_one = grad_one + part.astype(f32)
    high = list(range(1, bits))
    own_qkv = grad_w[1].astype(f32) + turned_w.astype(f32)
    own_qkv = own_qkv.reshape(*[2] * (bits - 1), *own_qkv.shape[1:])
    send, keep_w = scatter_step(own_qkv, high, 1)
    came_w = hop(send, "seq", 2)
    keep_m, came_m = (jnp.concatenate(part, axis=1) for part in zip(*parts_m))
    if bits > 2:
        own_qkv = keep_w.astype(f32) + came_w.astype(f32)
        keep_w, came_w = scatter_seq(own_qkv, high[1:], high[1:])
    cut = (width // 512) * 128
    to_last = [(i, i - 1) for i in range(1, n_seq)]
    rim_low = rim_one.astype(bf16)
    back = [lax.ppermute(part, "seq", to_last) for part in (rim_low[:, :cut], rim_low[:, cut:])]
    grad_one = grad_one + jnp.concatenate(back, axis=1).astype(f32)
    came_w = after(came_w, back[0], far_here)
    x_part = x_share.astype(f32)
    factor_one = lax.rsqrt(jnp.mean(x_part * x_part, axis=-1, keepdims=True) + EPSILON)
    norm_one = x_part * factor_one
    gain_one_grad = jnp.sum(grad_one * norm_one, axis=0)
    scaled = grad_one * gains[0]
    tokens_grad = grad_mid + factor_one * (
        scaled - norm_one * jnp.mean(scaled * norm_one, axis=-1, keepdims=True)
    )

    total_cols = cols_own * n_tensor
    shape_w = (sds((3, rows_own, cols_own), f32), sds((rows_own, cols_own), f32))
    shape_w = (*shape_w, sds((2, rows_own, cols_own), f32))
    *grads, col_part, row_part = vmem_call(
        grads_kernel,
        (*shape_w, sds((8, cols_own), f32), sds((8, rows_own), f32)),
        [],
        1e9,
        32,
        keep_w,
        came_w,
        keep_m,
        came_m,
    )
    col_new, row_new, unscaled, unscaled_part = vmem_call(
        functools.partial(update_kernel, (total_cols, width)),
        (
            sds((6, cols_own), f32),
            sds((6, rows_own), f32),
            sds((6, rows_own, cols_own), f32),
            sds((6, cols_own), f32),
        ),
        [],
        1e9,
        32,
        *grads,
        after(summed(col_part, "seq"), back),
        summed(row_part, "tensor"),
        col_second,
        row_second,
    )

    gain_part = jnp.stack([gain_one_grad, gain_two_grad[0]])
    gain_part = gain_part.reshape(2, n_seq, rows_own).transpose(1, 0, 2).reshape(n_seq, 2 * rows_own)
    rest = jnp.concatenate(
        [
            scale_part,
            jnp.sum(unscaled_part, axis=1),
            jnp.sum(row_part[:6], axis=1),
            jnp.sum(row_second, axis=1) / n_tensor,
        ]
    )
    rest = jnp.broadcast_to(rest, (n_seq, HD + 18))
    last = jnp.concatenate([gain_part, rest], axis=1)
    size = -(-last.shape[1] // 1024) * 1024
    last = jnp.pad(last, ((0, 0), (0, size - last.shape[1]))).reshape(n_seq, 1, size // 128, 128)
    last = jnp.broadcast_to(last, (n_seq, n_tensor, size // 128, 128))
    last = last.reshape(n_seq * n_tensor, size // 128, 128)
    got = lax.all_to_all(last, ("seq", "tensor"), split_axis=0, concat_axis=0)
    gains_grad, scale_grad, unscaled_square, all_square, old_sums = unpacked(
        jnp.sum(got, axis=0), (2, rows_own), (HD,), (6,), (6,), (6,)
    )
    row_mean = (BETA_TWO * old_sums + (1.0 - BETA_TWO) * all_square / total_cols) / width
    update_rms = jnp.sqrt(row_mean * unscaled_square / (width * total_cols))
    step = STEP_RATE * jnp.sqrt(row_mean) / jnp.maximum(1.0, update_rms / CLIP_LEVEL)
    fresh = vmem_call(
        step_kernel,
        shape_w,
        [],
        1e9,
        32,
        unscaled,
        jnp.broadcast_to(step[:, None], (6, cols_own)),
        qkv,
        out_proj,
        mlp,
    )
    gains_own = lax.dynamic_slice_in_dim(gains, seq_index * rows_own, rows_own, 1)
    gain_second_new = BETA_TWO * gain_second + (1.0 - BETA_TWO) * gains_grad * gains_grad
    gains_new = gains_own - VECTOR_RATE * gains_grad * lax.rsqrt(gain_second_new)
    scale_second_new = BETA_TWO * scale_second + (1.0 - BETA_TWO) * scale_grad * scale_grad
    scale_new = query_scale - VECTOR_RATE * scale_grad * lax.rsqrt(scale_second_new)
    return (
        result,
        tokens_grad,
        *grads,
        gains_grad,
        scale_grad,
        *fresh,
        gains_new,
        scale_new,
        row_new,
        col_new,
        update_rms,
        gain_second_new,
        scale_second_new,
    )


def solution(mesh):
    return jax.shard_map(
        shards,
        mesh=mesh,
        in_specs=(
            P("seq", None),
            P(("seq", "tensor"), None),
            P(),
            P(None, "seq", "tensor"),
            P("seq", "tensor"),
            P(None, "seq", "tensor"),
            P(),
            P(),
            P(None, "seq"),
            P(None, "tensor"),
            P(None, "seq"),
            P(),
        ),
        out_specs=(
            P(("seq", "tensor"), None),
            P(("seq", "tensor"), None),
            P(None, "seq", "tensor"),
            P("seq", "tensor"),
            P(None, "seq", "tensor"),
            P(None, "seq"),
            P(),
            P(None, "seq", "tensor"),
            P("seq", "tensor"),
            P(None, "seq", "tensor"),
            P(None, "seq"),
            P(),
            P(None, "seq"),
            P(None, "tensor"),
            P(),
            P(None, "seq"),
            P(),
        ),
        check_vma=False,
    )
```

```python
import functools
import math

import jax
import jax.numpy as jnp
from jax import lax
from jax.experimental import pallas as pl
from jax.experimental.pallas import tpu as pltpu
from jax.sharding import PartitionSpec as P

HD = 80
WINDOW = 1024
BLOCK = 256
SPAN = WINDOW + BLOCK
LANES = 128

EPSILON = 1e-06
LOG_BASE = 1.442695
BETA_TWO = 0.5
STEP_RATE = 0.3
CLIP_LEVEL = 0.1
VECTOR_RATE = 0.3
NEGATIVE = -1e30
SCALE_ROOT = LOG_BASE / math.sqrt(HD)
MIB = 1024 * 1024

bf16 = jnp.bfloat16
f32 = jnp.float32


def dot(left, right, dims):
    return lax.dot_general(left, right, (dims, ((), ())), preferred_element_type=f32)


def vmem_call(body, outs, scratch, flops, limit, *args, far_in=(), far_out=()):
    size = sum(math.prod(a.shape) * a.dtype.itemsize for a in (*args, *outs))
    space = pl.BlockSpec(memory_space=pltpu.VMEM)
    scalars = pl.BlockSpec(memory_space=pltpu.SMEM)
    anywhere = pl.BlockSpec(memory_space=pl.ANY)
    return pl.pallas_call(
        body,
        out_shape=outs,
        in_specs=[
            scalars if a.ndim == 1 else anywhere if i in far_in else space
            for i, a in enumerate(args)
        ],
        out_specs=[anywhere if i in far_out else space for i in range(len(outs))],
        scratch_shapes=scratch,
        compiler_params=pltpu.CompilerParams(vmem_limit_bytes=limit * MIB),
        cost_estimate=pl.CostEstimate(flops=8 * int(flops), bytes_accessed=size, transcendentals=0),
    )(*args)


def hop(value, axis, flip):
    peers = lax.axis_size(axis)
    return lax.ppermute(value, axis, [(i, i ^ flip) for i in range(peers)])


def after(value, *earlier):
    return lax.optimization_barrier((value, *earlier))[0]


def put(table, piece, row):
    return lax.dynamic_update_slice_in_dim(table, piece, row, 0)


def in_order(piece, other):
    low = lax.axis_index("seq") % 2 == 0
    return jnp.concatenate([jnp.where(low, piece, other), jnp.where(low, other, piece)], axis=0)


def gather_pairs(shard, other, first, second):
    peers = lax.axis_size("seq")
    pairs = {0: in_order(shard, other)}
    for f in range(2, peers // 2, 2):
        piece = after(hop(after(shard, first), "seq", 2 * f), first)
        pairs[f] = in_order(piece, hop(piece, "seq", 1))
    for f in range(0, peers // 2, 2):
        pairs[f + 1] = hop(after(pairs[f], second(f, pairs)), "seq", 2)
    return pairs


def gather_groups(shard):
    peers = lax.axis_size("seq")
    evens = list(range(0, peers // 2, 2))
    groups = [shard[None]]
    if evens[1:]:
        groups.append(jnp.stack([hop(shard, "seq", 2 * f) for f in evens[1:]]))
    others = [hop(group, "seq", 1) for group in groups]
    groups.append(hop(jnp.concatenate(groups, axis=0), "seq", 2))
    others.append(hop(groups[-1], "seq", 1))
    return groups, others, evens + [f + 1 for f in evens]


def scatter_step(total, left, k):
    at = len(left) - 1 - left.index(k)
    bit = (lax.axis_index("seq") >> k) & 1
    send = lax.dynamic_index_in_dim(total, 1 - bit, at, keepdims=False).astype(bf16)
    return send, lax.dynamic_index_in_dim(total, bit, at, keepdims=False)


def scatter_seq(total, left, order, *earlier):
    left = list(left)
    for k in order:
        send, keep = scatter_step(total, left, k)
        send = after(send, *earlier) if len(left) == 1 else send
        left.remove(k)
        came = hop(send, "seq", 1 << k)
        if left:
            total = keep.astype(f32) + came.astype(f32)
    return keep, came


def summed(value, axis):
    flip = 1
    while flip < lax.axis_size(axis):
        value = value + hop(value, axis, flip)
        flip *= 2
    return value


def packed(*values):
    flat = jnp.concatenate([v.reshape(-1) for v in values])
    size = -(-flat.shape[0] // 1024) * 1024
    return jnp.pad(flat, (0, size - flat.shape[0])).reshape(size // 128, 128)


def unpacked(table, *shapes):
    flat, out, at = table.reshape(-1), [], 0
    for shape in shapes:
        size = math.prod(shape)
        out.append(flat[at : at + size].reshape(shape))
        at += size
    return out


def head_of(rows, h):
    zeros = jnp.zeros((rows.shape[0], LANES - HD), rows.dtype)
    return jnp.concatenate([rows[:, h * HD : (h + 1) * HD], zeros], axis=1)


def attend_kernel(heads, counts, *refs):
    n_near, n_rim, n_parts = counts
    refs = list(refs)

    def take(n):
        out = refs[:n]
        del refs[:n]
        return out

    at_ref, tok_in = take(2)
    rims, near, far = take(n_rim), take(n_near), take(n_near)
    gain_ref, sc_ref, lo_ref = take(3)
    h_out, q_out, k_out, v_out, w_out, lse_ref = take(6)
    pieces = take(n_parts)
    x_ref, h_ref, w_ref, q_ref, k_ref, v_ref, kh, vt, bias, c_ref = take(10)
    stages, (in_sem, out_sem) = take(2 * n_near), take(2)
    cols = heads * HD
    rows = q_ref.shape[0]

    arrive = []

    def bring(source, target):
        arrive.append(pltpu.make_async_copy(source, target, in_sem.at[len(arrive)]))
        arrive[-1].start()
        return arrive[-1]

    weights = [bring(a, b) for a, b in zip((*near, *far), stages)]
    own = bring(tok_in, x_ref.at[pl.ds(WINDOW, rows), :])
    spot = 1 + sum(a.shape[0] for a in near)
    rim_copies = []
    for i, rim in enumerate(rims):
        place = pl.multiple_of(at_ref[spot + i], 16)
        rim_copies.append(bring(rim, x_ref.at[pl.ds(place, rim.shape[0]), :]))
    spot += n_rim

    leave = []

    def send(source, target):
        leave.append(pltpu.make_async_copy(source, target, out_sem.at[len(leave)]))
        leave[-1].start()

    for copy in weights:
        copy.wait()
    turn = 1
    for one, two in zip(stages[:n_near], stages[n_near:]):
        for i in range(one.shape[0]):
            at = pl.ds(pl.multiple_of(at_ref[turn], 16), 2 * one.shape[1])
            turn += 1

            @pl.when(at_ref[0] == 0)
            def _():
                w_ref[at, :] = jnp.concatenate([one[i], two[i]], axis=0)

            @pl.when(at_ref[0] == 1)
            def _():
                w_ref[at, :] = jnp.concatenate([two[i], one[i]], axis=0)

    send(w_ref, w_out)

    blocks = h_ref.shape[0] // BLOCK
    own.wait()
    for j in range(blocks):
        i = (j + WINDOW // BLOCK) % blocks
        if i == 0:
            for copy in rim_copies:
                copy.wait()
        at = slice(i * BLOCK, (i + 1) * BLOCK)
        values = x_ref[at, :].astype(f32)
        factor = lax.rsqrt(jnp.mean(values * values, axis=-1, keepdims=True) + EPSILON)
        normed = (values * factor * gain_ref[...]).astype(bf16)
        h_ref[at, :] = normed
        proj = dot(normed, w_ref[:, : 3 * cols], ((1,), (0,)))
        if i * BLOCK >= WINDOW:
            q_ref[i * BLOCK - WINDOW : (i + 1) * BLOCK - WINDOW, :] = (
                proj[:, :cols] * sc_ref[...]
            ).astype(bf16)
        k_rows = proj[:, cols : 2 * cols].astype(bf16)
        v_rows = proj[:, 2 * cols :].astype(bf16)
        k_ref[at, :] = k_rows
        v_ref[at, :] = v_rows
        vt[:, at] = v_rows.T
        for h in range(heads):
            kh[h, at, :] = head_of(k_rows, h)
    for source, target in ((h_ref, h_out), (q_ref, q_out), (k_ref, k_out), (v_ref, v_out)):
        send(source, target)

    steps = [(b, h) for b in range(rows // BLOCK) for h in range(heads)]

    def begin(b, h):
        if h == 0:
            fill_bias(bias, b, lo_ref)
        keys = slice(b * BLOCK, b * BLOCK + SPAN)
        q_head = head_of(q_ref[b * BLOCK : (b + 1) * BLOCK, :], h)
        return dot(kh[h, keys, :], q_head, ((1,), (1,))) + bias[b % 2]

    ready, mixed = begin(*steps[0]), []
    for i, (b, h) in enumerate(steps):
        s = ready
        if i + 1 < len(steps):
            ready = begin(*steps[i + 1])
        at, keys = slice(b * BLOCK, (b + 1) * BLOCK), slice(b * BLOCK, b * BLOCK + SPAN)
        top = jnp.max(s, axis=0, keepdims=True)
        p = jnp.exp(s - top)
        total = jnp.sum(p, axis=0, keepdims=True)
        part = dot(vt[h * HD : (h + 1) * HD, keys], p.astype(bf16), ((1,), (0,)))
        mixed.append((part / total).T)
        lse_ref[h : h + 1, at] = top + jnp.log(total)
        if h == heads - 1:
            c_ref[at, :] = jnp.concatenate(mixed, axis=1).astype(bf16)
            mixed = []
    for i, piece in enumerate(pieces):
        share = piece.shape[0]
        piece[...] = c_ref[pl.ds(pl.multiple_of(at_ref[spot + i], 16), share), :]
    for copy in leave:
        copy.wait()


def fill_bias(bias, b, lo_ref):
    k_place = b * BLOCK + lax.broadcasted_iota(jnp.int32, (SPAN, BLOCK), 0)
    q_place = b * BLOCK + WINDOW + lax.broadcasted_iota(jnp.int32, (SPAN, BLOCK), 1)
    seen = (k_place >= lo_ref[:, b * BLOCK : (b + 1) * BLOCK]) & (k_place <= q_place)
    bias[b % 2] = jnp.where(seen, 0.0, NEGATIVE)


def attend_back_kernel(heads, n_parts, at_ref, *refs):
    parts = refs[:n_parts]
    q_ref, k_ref, v_ref, sc_ref, lo_ref, lse_ref, h_ref = refs[n_parts : n_parts + 7]
    outs = refs[n_parts + 7 :]
    dq_ref, dkv_ref, part_ref = outs[:3]
    send_ref, keep_ref = outs[3:5]
    kh, vh, kt, ht, g_ref, dk, dv, bias, h_rows, sem = outs[5:]
    arrive = pltpu.make_async_copy(h_ref, h_rows, sem)
    arrive.start()
    rows, cols = q_ref.shape
    for i, part in enumerate(parts):
        share = part.shape[0]
        g_ref[pl.ds(pl.multiple_of(at_ref[1 + i], 16), share), :] = part[...]
    kt[...] = k_ref[...].T
    for h in range(heads):
        kh[h] = head_of(k_ref[...], h)
        vh[h] = head_of(v_ref[...], h)
    part_ref[...] = jnp.zeros_like(part_ref)

    steps = [(b, h) for b in range(rows // BLOCK) for h in range(heads)]

    def begin(b, h):
        if h == 0:
            fill_bias(bias, b, lo_ref)
        at, keys = slice(b * BLOCK, (b + 1) * BLOCK), slice(b * BLOCK, b * BLOCK + SPAN)
        q_head, g_head = head_of(q_ref[at, :], h), head_of(g_ref[at, :], h)
        s = dot(kh[h, keys, :], q_head, ((1,), (1,))) + bias[b % 2]
        return s, dot(vh[h, keys, :], g_head, ((1,), (1,))), q_head, g_head

    ready, grads = begin(*steps[0]), []
    for i, (b, h) in enumerate(steps):
        s, dp, q_head, g_head = ready
        if i + 1 < len(steps):
            ready = begin(*steps[i + 1])
        at, keys = slice(b * BLOCK, (b + 1) * BLOCK), slice(b * BLOCK, b * BLOCK + SPAN)
        p = jnp.exp(s - lse_ref[h : h + 1, at])
        inner = jnp.sum(p * dp, axis=0, keepdims=True)
        ds = (p * (dp - inner)).astype(bf16)
        g_value, g_key = dot(p.astype(bf16), g_head, ((1,), (0,))), dot(ds, q_head, ((1,), (0,)))
        for table, part in ((dv, g_value), (dk, g_key)):
            if b:
                table[h, b * BLOCK : b * BLOCK + WINDOW, :] += part[:WINDOW]
                table[h, b * BLOCK + WINDOW : b * BLOCK + SPAN, :] = part[WINDOW:]
            else:
                table[h, keys, :] = part
        grads.append(dot(kt[h * HD : (h + 1) * HD, keys], ds, ((1,), (0,))).T)
        if h == heads - 1:
            grad, grads = jnp.concatenate(grads, axis=1), []
            part_ref[...] += jnp.sum(grad * q_ref[at, :].astype(f32), axis=0, keepdims=True)
            dq_ref[at, :] = (grad * sc_ref[...]).astype(bf16)
    arrive.wait()
    for i in range(k_ref.shape[0] // BLOCK):
        at = pl.ds(i * BLOCK, BLOCK)
        both = [table[h, at, :HD] for table in (dk, dv) for h in range(heads)]
        dkv_ref[at, :] = jnp.concatenate(both, axis=1).astype(bf16)
        ht[:, at] = h_rows[at, :].T
    gw_q = dot(ht[:, WINDOW:], dq_ref[...], ((1,), (0,))).astype(bf16)
    gw_kv = dot(ht[...], dkv_ref[...], ((1,), (0,))).astype(bf16)
    outer, own, padded = send_ref.shape
    zeros = jnp.zeros((2 * outer * own, padded - 3 * cols), bf16)
    whole = jnp.concatenate([gw_q, gw_kv, zeros], axis=1)
    for low in range(2):

        @pl.when(at_ref[0] == low)
        def _():
            for i in range(2 * outer):
                to = keep_ref if i % 2 == low else send_ref
                to[i // 2] = whole[i * own : (i + 1) * own]


def rows_kernel(parts, at_ref, q_ref, kv_ref, w_ref, even_ref, odd_ref):
    cols, width = q_ref.shape[1], w_ref.shape[0]
    share = even_ref.shape[1]
    for f in range(parts):
        at = pl.multiple_of(at_ref[f], 16)
        here = pl.ds(pl.multiple_of(at + WINDOW, 16), share)
        to = odd_ref if f % 2 else even_ref
        grads = jnp.concatenate([q_ref[pl.ds(at, share), :], kv_ref[here, :]], axis=1)
        to[f // 2, :, width:] = dot(grads, w_ref[:, : 3 * cols], ((1,), (1,))).astype(bf16)
        to[f // 2, :, :width] = dot(
            kv_ref[pl.ds(at, share), :], w_ref[:, cols : 3 * cols], ((1,), (1,))
        ).astype(bf16)


def rows_kernel(parts, at_ref, q_ref, kv_ref, w_ref, even_ref, odd_ref):
    cols, width = q_ref.shape[1], w_ref.shape[0]
    share = even_ref.shape[1]
    for f in range(parts):
        at = pl.multiple_of(at_ref[f], 16)
        here = pl.ds(pl.multiple_of(at + WINDOW, 16), share)
        to = odd_ref if f % 2 else even_ref
        grads = jnp.concatenate([q_ref[pl.ds(at, share), :], kv_ref[here, :]], axis=1)
        to[f // 2, :, width:] = dot(grads, w_ref[:, : 3 * cols], ((1,), (1,))).astype(bf16)
        to[f // 2, :, :width] = dot(
            kv_ref[pl.ds(at, share), :], w_ref[:, cols : 3 * cols], ((1,), (1,))
        ).astype(bf16)


def share_kernel(counts, at_ref, *refs):
    peers = len(counts)
    ctx, refs = refs[:peers], refs[peers:]
    mats = [refs[sum(counts[:r]) : sum(counts[: r + 1])] for r in range(peers)]
    refs = refs[sum(counts) :]
    x_ref, cot_ref, gain_ref = refs[:3]
    outs = refs[3:]
    res_ref, gmid_ref, part_ref, rows_ref, even_ref, odd_ref = outs[:6]
    gctx = outs[6 : 6 + peers]
    w_out, w_in, w_back = outs[6 + peers :]
    cols = ctx[0].shape[1]
    for r, pieces in enumerate(mats):
        for i, (m, k) in enumerate((m, k) for m in pieces for k in range(m.shape[0])):
            at = pl.ds(pl.multiple_of(at_ref[i], 16), m.shape[1])
            for j, w in enumerate((w_out, w_in, w_back)):
                w[at, r * cols : (r + 1) * cols] = m[k, :, j * cols : (j + 1) * cols]
    gain = gain_ref[...]
    mixed = jnp.concatenate([c[...] for c in ctx], axis=1)
    mid = x_ref[...].astype(f32) + dot(mixed, w_out[...], ((1,), (1,)))
    factor = lax.rsqrt(jnp.mean(mid * mid, axis=-1, keepdims=True) + EPSILON)
    normed = mid * factor
    h2 = (normed * gain).astype(bf16)
    rows_ref[1] = h2
    cot = cot_ref[...]
    pre = dot(h2, w_in[...], ((1,), (0,)))
    g_hid = dot(cot, w_back[...], ((1,), (0,)))
    sig = 1.0 / (1.0 + jnp.exp(-pre))
    hidden = (pre * sig).astype(bf16)
    g_pre = (g_hid * sig * (1.0 + pre * (1.0 - sig))).astype(bf16)
    for r in range(peers):
        half, to = odd_ref if r % 2 else even_ref, slice(r // 2 * cols, (r // 2 + 1) * cols)
        half[0, :, to] = g_pre[:, r * cols : (r + 1) * cols]
        half[1, :, to] = hidden[:, r * cols : (r + 1) * cols]
    res_ref[...] = mid + dot(hidden, w_back[...], ((1,), (1,)))
    g_h2 = dot(g_pre, w_in[...], ((1,), (1,)))
    part_ref[...] = jnp.sum(g_h2 * normed, axis=0, keepdims=True)
    scaled = g_h2 * gain
    back = factor * (scaled - normed * jnp.mean(scaled * normed, axis=-1, keepdims=True))
    g_mid = cot.astype(f32) + back
    gmid_ref[...] = g_mid
    gm = g_mid.astype(bf16)
    rows_ref[0] = gm
    g_mixed = dot(gm, w_out[...], ((1,), (0,))).astype(bf16)
    for r, out in enumerate(gctx):
        out[...] = g_mixed[:, r * cols : (r + 1) * cols]


def share_grads_kernel(count, at_ref, *refs):
    ctx, ctx_far = refs[:count], refs[count]
    rows_ref, rows_far, even_ref, odd_far, cot_ref, cot_far = refs[count + 1 : count + 7]
    firsts, send_ref, keep_ref = refs[count + 7 : 2 * count + 7], *refs[2 * count + 7 :]
    lefts = [
        jnp.concatenate([one.T, two.T], axis=1)
        for one, two in (
            (rows_ref[0], rows_far[0]),
            (rows_ref[1], rows_far[1]),
            (cot_ref[...], cot_far[...]),
        )
    ]
    half, cols = firsts[0].shape[-1], ctx[0].shape[1]
    zeros = jnp.zeros((firsts[0].shape[0], 2 * half - 3 * cols), bf16)
    pairs, rows = send_ref.shape[1:3]
    for r in range(count):
        to = slice(r * cols, (r + 1) * cols)
        rights = (
            (ctx[r][...], ctx_far[:, to]),
            (even_ref[0, :, to], odd_far[0, :, to]),
            (even_ref[1, :, to], odd_far[1, :, to]),
        )
        parts = [
            dot(left, jnp.concatenate(right, axis=0), ((1,), (0,))).astype(bf16)
            for left, right in zip(lefts, rights)
        ]
        whole = jnp.concatenate([*parts, zeros], axis=1)
        firsts[r][...] = whole[:, :half]
        for bit, (zero, one) in enumerate(((keep_ref, send_ref), (send_ref, keep_ref))):

            @pl.when(at_ref[0] == bit)
            def _():
                for i in range(pairs):
                    zero[r, i] = whole[2 * i * rows : (2 * i + 1) * rows, half:]
                    one[r, i] = whole[(2 * i + 1) * rows : (2 * i + 2) * rows, half:]


def grads_kernel(keep_w, came_w, keep_m, came_m, qkv_ref, out_ref, mlp_ref, col_ref, row_ref):
    cols = out_ref.shape[1]
    col_ref[...] = jnp.zeros_like(col_ref)
    row_sums = []
    for i, (keep, came) in enumerate(((keep_w, came_w), (keep_m, came_m))):
        total = keep[...].astype(f32) + came[...].astype(f32)
        for j in range(3):
            grad = total[:, j * cols : (j + 1) * cols]
            if i == 0:
                qkv_ref[j] = grad
            elif j == 0:
                out_ref[...] = grad
            else:
                mlp_ref[j - 1] = grad
            square = grad * grad
            col_ref[3 * i + j : 3 * i + j + 1, :] = jnp.sum(square, axis=0, keepdims=True)
            row_sums.append(jnp.sum(square, axis=1, keepdims=True))
    zeros = jnp.zeros((row_sums[0].shape[0], LANES - 6), f32)
    row_ref[...] = jnp.concatenate([*row_sums, zeros], axis=1).T[:8, :]


def update_kernel(sizes, qkv_ref, out_ref, mlp_ref, col_ref, row_ref, cs_ref, rs_ref, cn_ref, rn_ref, up_ref, sq_ref):
    total_cols, width = sizes
    col_new = BETA_TWO * cs_ref[...] + (1.0 - BETA_TWO) * col_ref[:6, :] / width
    row_new = BETA_TWO * rs_ref[...] + (1.0 - BETA_TWO) * row_ref[:6, :] / total_cols
    cn_ref[...] = col_new
    rn_ref[...] = row_new
    rows = row_new.shape[1]
    row_cols = jnp.concatenate([row_new, jnp.ones((2, rows), f32)], axis=0).T
    sq_ref[...] = jnp.zeros_like(sq_ref)
    for i in range(6):
        grad = qkv_ref[i] if i < 3 else out_ref[...] if i == 3 else mlp_ref[i - 4]
        update = grad * lax.rsqrt(row_cols[:, i : i + 1] * col_new[i : i + 1, :])
        up_ref[i] = update
        sq_ref[i : i + 1, :] = jnp.sum(update * update, axis=0, keepdims=True)


def step_kernel(up_ref, step_ref, qkv_ref, out_ref, mlp_ref, qkv_new, out_new, mlp_new):
    for i in range(6):
        old, new = (qkv_ref, qkv_new) if i < 3 else (mlp_ref, mlp_new)
        change = step_ref[i : i + 1, :] * up_ref[i]
        if i == 3:
            out_new[...] = out_ref[...] - change
        else:
            new[i % 4] = old[i % 4] - change


def shards(
    tokens,
    cotangent,
    lengths,
    qkv,
    out_proj,
    mlp,
    gains,
    query_scale,
    row_second,
    col_second,
    gain_second,
    scale_second,
):
    n_tensor, n_seq = lax.axis_size("tensor"), lax.axis_size("seq")
    seq_index, ten_index = lax.axis_index("seq"), lax.axis_index("tensor")
    tok_dev, width = tokens.shape
    share = cotangent.shape[0]
    rows_own, cols_own = qkv.shape[1], qkv.shape[2]
    heads = cols_own // HD
    row_first = ten_index * share
    flips = list(range(n_tensor))
    sds = jax.ShapeDtypeStruct

    x_share = lax.dynamic_slice_in_dim(tokens, row_first, share, 0)

    padded = -(-3 * cols_own // 256) * 256
    fill = jnp.zeros((rows_own, padded - 3 * cols_own), f32)
    shard_m = jnp.concatenate([out_proj, mlp[0], mlp[1], fill], axis=1).astype(bf16)
    shard_qkv = jnp.concatenate([qkv[0], qkv[1], qkv[2], fill], axis=1).astype(bf16)
    near, far, flips_q = gather_groups(shard_qkv)
    rim_own = lax.ppermute(x_share, "seq", [(i, i + 1) for i in range(n_seq - 1)])
    rims = [rim_own] + [hop(rim_own, "tensor", f) for f in flips[2::2]]
    flips_rim = flips[::2] + flips[1::2]
    rims = rims + [hop(piece, "tensor", 1) for piece in rims]
    across = {f: {} for f in flips[2::2]}

    def send_across(g, pairs, *earlier):
        for f in across:
            across[f][g] = hop(after(pairs[g], *earlier), "tensor", f)
        return [across[f][g] for f in across]

    other_m = hop(after(shard_m, far[0]), "seq", 1)
    own_across = {f: hop(shard_m, "tensor", f) for f in across}

    def second(f, pairs):
        if not f:
            for g in across:
                across[g][0] = in_order(own_across[g], hop(other_m, "tensor", g))
            return near[-1], far[1]
        return send_across(f, pairs, rims[: n_tensor // 2])

    pairs_m = gather_pairs(shard_m, other_m, (near[1], far[0], list(own_across.values())), second)
    for g in pairs_m:
        if g % 2:
            send_across(g, pairs_m, list(across[flips[2]].values())[-1])
    flips_m = list(pairs_m)
    mats = {0: [jnp.stack([pairs_m[g] for g in flips_m])]}
    mats[1] = [hop(mats[0][0], "tensor", 1)]
    for f in across:
        mats[f] = [across[f][g][None] for g in flips_m]
    low, outer = seq_index % 2, seq_index // 2
    spots_share = [(ten_index ^ f) * share for f in flips]
    spots_q = [(outer ^ f) * 2 * rows_own for f in flips_q]
    spots_rim = [(ten_index ^ f) * share for f in flips_rim]
    spots_m = [(outer ^ f) * 2 * rows_own for f in flips_m]

    places = seq_index * tok_dev + jnp.arange(tok_dev, dtype=jnp.int32)
    ends = jnp.cumsum(lengths[0])
    passed = ends[None, :] <= places[:, None]
    doc_start = jnp.max(jnp.where(passed, ends[None, :], 0), axis=1)
    lo = jnp.maximum(places - (WINDOW - 1), doc_start)
    lo = jnp.where(places >= ends[-1], places, lo)
    lo = (lo - (seq_index * tok_dev - WINDOW)).astype(jnp.int32)[None, :]

    factor = jax.nn.softplus(query_scale) * SCALE_ROOT
    scale_cols = jnp.tile(factor, heads)[None, :]
    table = WINDOW + tok_dev
    pair_flops = tok_dev * SPAN * cols_own * 2
    stages = [pltpu.VMEM(part.shape, bf16) for part in (*near, *far)]
    n_in = len(stages) + 1 + len(rims)
    h_all, queries, key_rows, value_rows, w_qkv, log_totals, *ctx = vmem_call(
        functools.partial(attend_kernel, heads, (len(near), len(rims), n_tensor)),
        (
            sds((table, width), bf16),
            sds((tok_dev, cols_own), bf16),
            sds((table, cols_own), bf16),
            sds((table, cols_own), bf16),
            sds((width, padded), bf16),
            sds((heads, tok_dev), f32),
            *[sds((share, cols_own), bf16) for _ in flips],
        ),
        [
            pltpu.VMEM((table, width), bf16),
            pltpu.VMEM((table, width), bf16),
            pltpu.VMEM((width, padded), bf16),
            pltpu.VMEM((tok_dev, cols_own), bf16),
            pltpu.VMEM((table, cols_own), bf16),
            pltpu.VMEM((table, cols_own), bf16),
            pltpu.VMEM((heads, table, LANES), bf16),
            pltpu.VMEM((cols_own, table), bf16),
            pltpu.VMEM((2, SPAN, BLOCK), f32),
            pltpu.VMEM((tok_dev, cols_own), bf16),
            *stages,
            pltpu.SemaphoreType.DMA((n_in,)),
            pltpu.SemaphoreType.DMA((5,)),
        ],
        2 * table * width * 3 * cols_own + 6 * pair_flops,
        56,
        jnp.stack([low, *spots_q, *spots_rim, *spots_share]),
        tokens,
        *rims,
        *near,
        *far,
        gains[:1],
        scale_cols,
        lo,
        far_in=range(1, 1 + n_in),
        far_out=range(5),
    )
    for f in flips[2::2]:
        mats[f + 1] = [hop(after(piece, log_totals), "tensor", 1) for piece in mats[f]]

    ctx = [ctx[0]] + [hop(ctx[f], "tensor", f) for f in flips[1:]]
    shape_share = (share, width)
    outs = vmem_call(
        functools.partial(share_kernel, [len(mats[f]) for f in flips]),
        (
            sds(shape_share, f32),
            sds(shape_share, f32),
            sds((1, width), f32),
            sds((2, share, width), bf16),
            sds((2, share, n_tensor // 2 * cols_own), bf16),
            sds((2, share, n_tensor // 2 * cols_own), bf16),
            *[sds((share, cols_own), bf16) for _ in flips],
        ),
        [pltpu.VMEM((width, width), bf16) for _ in range(3)],
        2 * 6 * share * width * width,
        44,
        jnp.stack(spots_m),
        *ctx,
        *[piece for f in flips for piece in mats[f]],
        x_share,
        cotangent,
        gains[1:],
    )
    result, grad_mid, gain_two_grad, rows_two, even, odd = outs[:6]
    gctx = outs[6:]
    gctx = [gctx[0]] + [hop(gctx[f], "tensor", f) for f in flips[1:]]

    n_even, half = n_tensor // 2, padded // 2
    halves = sds((n_even, n_seq // 4, 2 * rows_own, half), bf16)
    *firsts, send, keep = vmem_call(
        functools.partial(share_grads_kernel, n_even),
        (*[sds((width, half), bf16) for _ in range(n_even)], halves, halves),
        [],
        2 * 3 * share * width * width,
        44,
        (outer % 2)[None],
        *ctx[::2],
        hop(jnp.concatenate(ctx[1::2], axis=1), "tensor", 1),
        rows_two,
        hop(rows_two, "tensor", 1),
        even,
        hop(odd, "tensor", 1),
        cotangent,
        hop(cotangent, "tensor", 1),
    )
    came = [hop(part, "tensor", 2 * i) for i, part in enumerate(firsts) if i]
    turned = hop(send, "seq", 2)
    log_totals, _ = lax.optimization_barrier((log_totals, firsts + [send]))

    grad_q, grad_kv, scale_raw, *grad_w = vmem_call(
        functools.partial(attend_back_kernel, heads, n_tensor),
        (
            sds((tok_dev, cols_own), bf16),
            sds((table, 2 * cols_own), bf16),
            sds((1, cols_own), f32),
            *[sds((n_seq // 2, rows_own, padded), bf16) for _ in range(2)],
        ),
        [
            pltpu.VMEM((heads, table, LANES), bf16),
            pltpu.VMEM((heads, table, LANES), bf16),
            pltpu.VMEM((cols_own, table), bf16),
            pltpu.VMEM((width, table), bf16),
            pltpu.VMEM((tok_dev, cols_own), bf16),
            pltpu.VMEM((heads, table, LANES), f32),
            pltpu.VMEM((heads, table, LANES), f32),
            pltpu.VMEM((2, SPAN, BLOCK), f32),
            pltpu.VMEM((table, width), bf16),
            pltpu.SemaphoreType.DMA,
        ],
        14 * pair_flops + 2 * table * width * 3 * cols_own,
        56,
        jnp.stack([low, *spots_share]),
        *gctx,
        queries,
        key_rows,
        value_rows,
        scale_cols,
        lo,
        log_totals,
        h_all,
        far_in=[n_tensor + 7],
    )
    scale_part = (
        jnp.sum((scale_raw / scale_cols).reshape(heads, HD), axis=0)
        * SCALE_ROOT
        * jax.nn.sigmoid(query_scale)
    )
    bits = n_seq.bit_length() - 1
    part_rows = sds((n_even, share, 2 * width), bf16)
    even_rows, odd_rows = vmem_call(
        functools.partial(rows_kernel, n_tensor),
        (part_rows, part_rows),
        [],
        2 * (tok_dev * 5 * cols_own) * width,
        44,
        jnp.stack(spots_share),
        grad_q,
        grad_kv,
        w_qkv,
    )
    turned_w = hop(grad_w[0], "seq", 1)

    first = firsts[0].astype(f32)
    for part in came:
        first = first + part.astype(f32)
    first = first.reshape(*[2] * bits, rows_own, half)
    send, keep_first = scatter_step(first, list(range(bits)), 1)
    second = keep.astype(f32) + turned.astype(f32)
    sends = [second[i].astype(bf16) for i in range(1, n_even)]
    came_first = hop(send, "seq", 2)
    far_second = [hop(part, "tensor", 2 * i + 2) for i, part in enumerate(sends)]
    from_core_rows = hop(after(odd_rows, turned_w, came_first, far_second), "tensor", 1)
    sums = [even_rows[i].astype(f32) + from_core_rows[i].astype(f32) for i in range(n_even)]
    sum_sends = [part.astype(bf16) for part in sums[1:]]

    parts_m, rest = [], [0, *range(2, bits)]
    first = keep_first + came_first.astype(f32)
    second = second[0]
    for part in far_second:
        second = second + part.astype(f32)
    second = second.reshape(*[2] * (bits - 1), rows_own, half)
    for part, left, order in (
        (first, rest, rest),
        (second, rest, rest[::-1]),
    ):
        parts_m.append(scatter_seq(part, left, order))
    sum_sends = after(sum_sends, turned_w, far_second)
    far_rim = [hop(part[:, :width], "tensor", 2 * i + 2) for i, part in enumerate(sum_sends)]
    rim_one, grad_one = sums[0][:, :width], sums[0][:, width:]
    for part in far_rim:
        rim_one = rim_one + part.astype(f32)
    far_here = [
        hop(after(part[:, width:], far_rim), "tensor", 2 * i + 2)
        for i, part in enumerate(sum_sends)
    ]
    for part in far_here:
        grad_one = grad_one + part.astype(f32)
    high = list(range(1, bits))
    own_qkv = grad_w[1].astype(f32) + turned_w.astype(f32)
    own_qkv = own_qkv.reshape(*[2] * (bits - 1), *own_qkv.shape[1:])
    send, keep_w = scatter_step(own_qkv, high, 1)
    came_w = hop(send, "seq", 2)
    keep_m, came_m = (jnp.concatenate(part, axis=1) for part in zip(*parts_m))
    if bits > 2:
        own_qkv = keep_w.astype(f32) + came_w.astype(f32)
        keep_w, came_w = scatter_seq(own_qkv, high[1:], high[1:])
    cut = (width // 512) * 128
    to_last = [(i, i - 1) for i in range(1, n_seq)]
    rim_low = rim_one.astype(bf16)
    back = [lax.ppermute(part, "seq", to_last) for part in (rim_low[:, :cut], rim_low[:, cut:])]
    grad_one = grad_one + jnp.concatenate(back, axis=1).astype(f32)
    came_w = after(came_w, back[0], far_here)
    x_part = x_share.astype(f32)
    factor_one = lax.rsqrt(jnp.mean(x_part * x_part, axis=-1, keepdims=True) + EPSILON)
    norm_one = x_part * factor_one
    gain_one_grad = jnp.sum(grad_one * norm_one, axis=0)
    scaled = grad_one * gains[0]
    tokens_grad = grad_mid + factor_one * (
        scaled - norm_one * jnp.mean(scaled * norm_one, axis=-1, keepdims=True)
    )

    total_cols = cols_own * n_tensor
    shape_w = (sds((3, rows_own, cols_own), f32), sds((rows_own, cols_own), f32))
    shape_w = (*shape_w, sds((2, rows_own, cols_own), f32))
    *grads, col_part, row_part = vmem_call(
        grads_kernel,
        (*shape_w, sds((8, cols_own), f32), sds((8, rows_own), f32)),
        [],
        1e9,
        32,
        keep_w,
        came_w,
        keep_m,
        came_m,
    )
    col_new, row_new, unscaled, unscaled_part = vmem_call(
        functools.partial(update_kernel, (total_cols, width)),
        (
            sds((6, cols_own), f32),
            sds((6, rows_own), f32),
            sds((6, rows_own, cols_own), f32),
            sds((6, cols_own), f32),
        ),
        [],
        1e9,
        32,
        *grads,
        after(summed(col_part, "seq"), back),
        summed(row_part, "tensor"),
        col_second,
        row_second,
    )

    gain_part = jnp.stack([gain_one_grad, gain_two_grad[0]])
    gain_part = gain_part.reshape(2, n_seq, rows_own).transpose(1, 0, 2).reshape(n_seq, 2 * rows_own)
    rest = jnp.concatenate(
        [
            scale_part,
            jnp.sum(unscaled_part, axis=1),
            jnp.sum(row_part[:6], axis=1),
            jnp.sum(row_second, axis=1) / n_tensor,
        ]
    )
    rest = jnp.broadcast_to(rest, (n_seq, HD + 18))
    last = jnp.concatenate([gain_part, rest], axis=1)
    size = -(-last.shape[1] // 1024) * 1024
    last = jnp.pad(last, ((0, 0), (0, size - last.shape[1]))).reshape(n_seq, 1, size // 128, 128)
    last = jnp.broadcast_to(last, (n_seq, n_tensor, size // 128, 128))
    last = last.reshape(n_seq * n_tensor, size // 128, 128)
    got = lax.all_to_all(last, ("seq", "tensor"), split_axis=0, concat_axis=0)
    gains_grad, scale_grad, unscaled_square, all_square, old_sums = unpacked(
        jnp.sum(got, axis=0), (2, rows_own), (HD,), (6,), (6,), (6,)
    )
    row_mean = (BETA_TWO * old_sums + (1.0 - BETA_TWO) * all_square / total_cols) / width
    update_rms = jnp.sqrt(row_mean * unscaled_square / (width * total_cols))
    step = STEP_RATE * jnp.sqrt(row_mean) / jnp.maximum(1.0, update_rms / CLIP_LEVEL)
    fresh = vmem_call(
        step_kernel,
        shape_w,
        [],
        1e9,
        32,
        unscaled,
        jnp.broadcast_to(step[:, None], (6, cols_own)),
        qkv,
        out_proj,
        mlp,
    )
    gains_own = lax.dynamic_slice_in_dim(gains, seq_index * rows_own, rows_own, 1)
    gain_second_new = BETA_TWO * gain_second + (1.0 - BETA_TWO) * gains_grad * gains_grad
    gains_new = gains_own - VECTOR_RATE * gains_grad * lax.rsqrt(gain_second_new)
    scale_second_new = BETA_TWO * scale_second + (1.0 - BETA_TWO) * scale_grad * scale_grad
    scale_new = query_scale - VECTOR_RATE * scale_grad * lax.rsqrt(scale_second_new)
    return (
        result,
        tokens_grad,
        *grads,
        gains_grad,
        scale_grad,
        *fresh,
        gains_new,
        scale_new,
        row_new,
        col_new,
        update_rms,
        gain_second_new,
        scale_second_new,
    )


def solution(mesh):
    return jax.shard_map(
        shards,
        mesh=mesh,
        in_specs=(
            P("seq", None),
            P(("seq", "tensor"), None),
            P(),
            P(None, "seq", "tensor"),
            P("seq", "tensor"),
            P(None, "seq", "tensor"),
            P(),
            P(),
            P(None, "seq"),
            P(None, "tensor"),
            P(None, "seq"),
            P(),
        ),
        out_specs=(
            P(("seq", "tensor"), None),
            P(("seq", "tensor"), None),
            P(None, "seq", "tensor"),
            P("seq", "tensor"),
            P(None, "seq", "tensor"),
            P(None, "seq"),
            P(),
            P(None, "seq", "tensor"),
            P("seq", "tensor"),
            P(None, "seq", "tensor"),
            P(None, "seq"),
            P(),
            P(None, "seq"),
            P(None, "tensor"),
            P(),
            P(None, "seq"),
            P(),
        ),
        check_vma=False,
    )
```

```python
import functools
import math

import jax
import jax.numpy as jnp
from jax import lax
from jax.experimental import pallas as pl
from jax.experimental.pallas import tpu as pltpu
from jax.sharding import PartitionSpec as P

HD = 80
WINDOW = 1024
BLOCK = 256
SPAN = WINDOW + BLOCK
LANES = 128

EPSILON = 1e-06
LOG_BASE = 1.442695
BETA_TWO = 0.5
STEP_RATE = 0.3
CLIP_LEVEL = 0.1
VECTOR_RATE = 0.3
NEGATIVE = -1e30
SCALE_ROOT = LOG_BASE / math.sqrt(HD)
MIB = 1024 * 1024

bf16 = jnp.bfloat16
f32 = jnp.float32


def dot(left, right, dims):
    return lax.dot_general(left, right, (dims, ((), ())), preferred_element_type=f32)


def vmem_call(body, outs, scratch, flops, limit, *args, far_in=(), far_out=()):
    size = sum(math.prod(a.shape) * a.dtype.itemsize for a in (*args, *outs))
    space = pl.BlockSpec(memory_space=pltpu.VMEM)
    scalars = pl.BlockSpec(memory_space=pltpu.SMEM)
    anywhere = pl.BlockSpec(memory_space=pl.ANY)
    return pl.pallas_call(
        body,
        out_shape=outs,
        in_specs=[
            scalars if a.ndim == 1 else anywhere if i in far_in else space
            for i, a in enumerate(args)
        ],
        out_specs=[anywhere if i in far_out else space for i in range(len(outs))],
        scratch_shapes=scratch,
        compiler_params=pltpu.CompilerParams(vmem_limit_bytes=limit * MIB),
        cost_estimate=pl.CostEstimate(flops=8 * int(flops), bytes_accessed=size, transcendentals=0),
    )(*args)


def hop(value, axis, flip):
    peers = lax.axis_size(axis)
    return lax.ppermute(value, axis, [(i, i ^ flip) for i in range(peers)])


def after(value, *earlier):
    return lax.optimization_barrier((value, *earlier))[0]


def put(table, piece, row):
    return lax.dynamic_update_slice_in_dim(table, piece, row, 0)


def in_order(piece, other):
    low = lax.axis_index("seq") % 2 == 0
    return jnp.concatenate([jnp.where(low, piece, other), jnp.where(low, other, piece)], axis=0)


def gather_pairs(shard, other, first, second):
    peers = lax.axis_size("seq")
    pairs = {0: in_order(shard, other)}
    for f in range(2, peers // 2, 2):
        piece = after(hop(after(shard, first), "seq", 2 * f), first)
        pairs[f] = in_order(piece, hop(piece, "seq", 1))
    for f in range(0, peers // 2, 2):
        pairs[f + 1] = hop(after(pairs[f], second(f, pairs)), "seq", 2)
    return pairs


def gather_groups(shard):
    peers = lax.axis_size("seq")
    evens = list(range(0, peers // 2, 2))
    groups = [shard[None]]
    if evens[1:]:
        groups.append(jnp.stack([hop(shard, "seq", 2 * f) for f in evens[1:]]))
    others = [hop(group, "seq", 1) for group in groups]
    groups.append(hop(jnp.concatenate(groups, axis=0), "seq", 2))
    others.append(hop(groups[-1], "seq", 1))
    return groups, others, evens + [f + 1 for f in evens]


def scatter_step(total, left, k):
    at = len(left) - 1 - left.index(k)
    bit = (lax.axis_index("seq") >> k) & 1
    send = lax.dynamic_index_in_dim(total, 1 - bit, at, keepdims=False).astype(bf16)
    return send, lax.dynamic_index_in_dim(total, bit, at, keepdims=False)


def scatter_seq(total, left, order, *earlier):
    left = list(left)
    for k in order:
        send, keep = scatter_step(total, left, k)
        send = after(send, *earlier) if len(left) == 1 else send
        left.remove(k)
        came = hop(send, "seq", 1 << k)
        if left:
            total = keep.astype(f32) + came.astype(f32)
    return keep, came


def summed(value, axis):
    flip = 1
    while flip < lax.axis_size(axis):
        value = value + hop(value, axis, flip)
        flip *= 2
    return value


def packed(*values):
    flat = jnp.concatenate([v.reshape(-1) for v in values])
    size = -(-flat.shape[0] // 1024) * 1024
    return jnp.pad(flat, (0, size - flat.shape[0])).reshape(size // 128, 128)


def unpacked(table, *shapes):
    flat, out, at = table.reshape(-1), [], 0
    for shape in shapes:
        size = math.prod(shape)
        out.append(flat[at : at + size].reshape(shape))
        at += size
    return out


def head_of(rows, h):
    zeros = jnp.zeros((rows.shape[0], LANES - HD), rows.dtype)
    return jnp.concatenate([rows[:, h * HD : (h + 1) * HD], zeros], axis=1)


def attend_kernel(heads, counts, *refs):
    n_near, n_rim, n_parts = counts
    refs = list(refs)

    def take(n):
        out = refs[:n]
        del refs[:n]
        return out

    at_ref, tok_in = take(2)
    rims, near, far = take(n_rim), take(n_near), take(n_near)
    gain_ref, sc_ref, lo_ref = take(3)
    h_out, q_out, k_out, v_out, w_out, lse_ref = take(6)
    pieces = take(n_parts)
    x_ref, h_ref, w_ref, q_ref, k_ref, v_ref, kh, vt, bias, c_ref = take(10)
    stages, (in_sem, out_sem) = take(2 * n_near), take(2)
    cols = heads * HD
    rows = q_ref.shape[0]

    arrive = []

    def bring(source, target):
        arrive.append(pltpu.make_async_copy(source, target, in_sem.at[len(arrive)]))
        arrive[-1].start()
        return arrive[-1]

    weights = [bring(a, b) for a, b in zip((*near, *far), stages)]
    own = bring(tok_in, x_ref.at[pl.ds(WINDOW, rows), :])
    spot = 1 + sum(a.shape[0] for a in near)
    rim_copies = []
    for i, rim in enumerate(rims):
        place = pl.multiple_of(at_ref[spot + i], 16)
        rim_copies.append(bring(rim, x_ref.at[pl.ds(place, rim.shape[0]), :]))
    spot += n_rim

    leave = []

    def send(source, target):
        leave.append(pltpu.make_async_copy(source, target, out_sem.at[len(leave)]))
        leave[-1].start()

    for copy in weights:
        copy.wait()
    turn = 1
    for one, two in zip(stages[:n_near], stages[n_near:]):
        for i in range(one.shape[0]):
            at = pl.ds(pl.multiple_of(at_ref[turn], 16), 2 * one.shape[1])
            turn += 1

            @pl.when(at_ref[0] == 0)
            def _():
                w_ref[at, :] = jnp.concatenate([one[i], two[i]], axis=0)

            @pl.when(at_ref[0] == 1)
            def _():
                w_ref[at, :] = jnp.concatenate([two[i], one[i]], axis=0)

    send(w_ref, w_out)

    blocks = h_ref.shape[0] // BLOCK
    own.wait()
    for j in range(blocks):
        i = (j + WINDOW // BLOCK) % blocks
        if i == 0:
            for copy in rim_copies:
                copy.wait()
        at = slice(i * BLOCK, (i + 1) * BLOCK)
        values = x_ref[at, :].astype(f32)
        factor = lax.rsqrt(jnp.mean(values * values, axis=-1, keepdims=True) + EPSILON)
        normed = (values * factor * gain_ref[...]).astype(bf16)
        h_ref[at, :] = normed
        proj = dot(normed, w_ref[:, : 3 * cols], ((1,), (0,)))
        if i * BLOCK >= WINDOW:
            q_ref[i * BLOCK - WINDOW : (i + 1) * BLOCK - WINDOW, :] = (
                proj[:, :cols] * sc_ref[...]
            ).astype(bf16)
        k_rows = proj[:, cols : 2 * cols].astype(bf16)
        v_rows = proj[:, 2 * cols :].astype(bf16)
        k_ref[at, :] = k_rows
        v_ref[at, :] = v_rows
        vt[:, at] = v_rows.T
        for h in range(heads):
            kh[h, at, :] = head_of(k_rows, h)
    for source, target in ((h_ref, h_out), (q_ref, q_out), (k_ref, k_out), (v_ref, v_out)):
        send(source, target)

    steps = [(b, h) for b in range(rows // BLOCK) for h in range(heads)]

    def begin(b, h):
        if h == 0:
            fill_bias(bias, b, lo_ref)
        keys = slice(b * BLOCK, b * BLOCK + SPAN)
        q_head = head_of(q_ref[b * BLOCK : (b + 1) * BLOCK, :], h)
        return dot(kh[h, keys, :], q_head, ((1,), (1,))) + bias[b % 2]

    ready, mixed = begin(*steps[0]), []
    for i, (b, h) in enumerate(steps):
        s = ready
        if i + 1 < len(steps):
            ready = begin(*steps[i + 1])
        at, keys = slice(b * BLOCK, (b + 1) * BLOCK), slice(b * BLOCK, b * BLOCK + SPAN)
        top = jnp.max(s, axis=0, keepdims=True)
        p = jnp.exp(s - top)
        total = jnp.sum(p, axis=0, keepdims=True)
        part = dot(vt[h * HD : (h + 1) * HD, keys], p.astype(bf16), ((1,), (0,)))
        mixed.append((part / total).T)
        lse_ref[h : h + 1, at] = top + jnp.log(total)
        if h == heads - 1:
            c_ref[at, :] = jnp.concatenate(mixed, axis=1).astype(bf16)
            mixed = []
    for i, piece in enumerate(pieces):
        share = piece.shape[0]
        piece[...] = c_ref[pl.ds(pl.multiple_of(at_ref[spot + i], 16), share), :]
    for copy in leave:
        copy.wait()


def fill_bias(bias, b, lo_ref):
    k_place = b * BLOCK + lax.broadcasted_iota(jnp.int32, (SPAN, BLOCK), 0)
    q_place = b * BLOCK + WINDOW + lax.broadcasted_iota(jnp.int32, (SPAN, BLOCK), 1)
    seen = (k_place >= lo_ref[:, b * BLOCK : (b + 1) * BLOCK]) & (k_place <= q_place)
    bias[b % 2] = jnp.where(seen, 0.0, NEGATIVE)


def attend_back_kernel(heads, n_parts, at_ref, *refs):
    parts = refs[:n_parts]
    q_ref, k_ref, v_ref, sc_ref, lo_ref, lse_ref, h_ref = refs[n_parts : n_parts + 7]
    outs = refs[n_parts + 7 :]
    dq_ref, dkv_ref, part_ref = outs[:3]
    send_ref, keep_ref = outs[3:5]
    kh, vh, kt, ht, g_ref, dk, dv, bias, h_rows, sem = outs[5:]
    arrive = pltpu.make_async_copy(h_ref, h_rows, sem)
    arrive.start()
    rows, cols = q_ref.shape
    for i, part in enumerate(parts):
        share = part.shape[0]
        g_ref[pl.ds(pl.multiple_of(at_ref[1 + i], 16), share), :] = part[...]
    kt[...] = k_ref[...].T
    for h in range(heads):
        kh[h] = head_of(k_ref[...], h)
        vh[h] = head_of(v_ref[...], h)
    part_ref[...] = jnp.zeros_like(part_ref)

    steps = [(b, h) for b in range(rows // BLOCK) for h in range(heads)]

    def begin(b, h):
        if h == 0:
            fill_bias(bias, b, lo_ref)
        at, keys = slice(b * BLOCK, (b + 1) * BLOCK), slice(b * BLOCK, b * BLOCK + SPAN)
        q_head, g_head = head_of(q_ref[at, :], h), head_of(g_ref[at, :], h)
        s = dot(kh[h, keys, :], q_head, ((1,), (1,))) + bias[b % 2]
        return s, dot(vh[h, keys, :], g_head, ((1,), (1,))), q_head, g_head

    ready, grads = begin(*steps[0]), []
    for i, (b, h) in enumerate(steps):
        s, dp, q_head, g_head = ready
        if i + 1 < len(steps):
            ready = begin(*steps[i + 1])
        at, keys = slice(b * BLOCK, (b + 1) * BLOCK), slice(b * BLOCK, b * BLOCK + SPAN)
        p = jnp.exp(s - lse_ref[h : h + 1, at])
        inner = jnp.sum(p * dp, axis=0, keepdims=True)
        ds = (p * (dp - inner)).astype(bf16)
        g_value, g_key = dot(p.astype(bf16), g_head, ((1,), (0,))), dot(ds, q_head, ((1,), (0,)))
        for table, part in ((dv, g_value), (dk, g_key)):
            if b:
                table[h, b * BLOCK : b * BLOCK + WINDOW, :] += part[:WINDOW]
                table[h, b * BLOCK + WINDOW : b * BLOCK + SPAN, :] = part[WINDOW:]
            else:
                table[h, keys, :] = part
        grads.append(dot(kt[h * HD : (h + 1) * HD, keys], ds, ((1,), (0,))).T)
        if h == heads - 1:
            grad, grads = jnp.concatenate(grads, axis=1), []
            part_ref[...] += jnp.sum(grad * q_ref[at, :].astype(f32), axis=0, keepdims=True)
            dq_ref[at, :] = (grad * sc_ref[...]).astype(bf16)
    arrive.wait()
    for i in range(k_ref.shape[0] // BLOCK):
        at = pl.ds(i * BLOCK, BLOCK)
        both = [table[h, at, :HD] for table in (dk, dv) for h in range(heads)]
        dkv_ref[at, :] = jnp.concatenate(both, axis=1).astype(bf16)
        ht[:, at] = h_rows[at, :].T
    gw_q = dot(ht[:, WINDOW:], dq_ref[...], ((1,), (0,))).astype(bf16)
    gw_kv = dot(ht[...], dkv_ref[...], ((1,), (0,))).astype(bf16)
    outer, own, padded = send_ref.shape
    zeros = jnp.zeros((2 * outer * own, padded - 3 * cols), bf16)
    whole = jnp.concatenate([gw_q, gw_kv, zeros], axis=1)
    for low in range(2):

        @pl.when(at_ref[0] == low)
        def _():
            for i in range(2 * outer):
                to = keep_ref if i % 2 == low else send_ref
                to[i // 2] = whole[i * own : (i + 1) * own]


def rows_kernel(parts, at_ref, q_ref, kv_ref, w_ref, even_ref, odd_ref):
    cols, width = q_ref.shape[1], w_ref.shape[0]
    share = even_ref.shape[1]
    for f in range(parts):
        at = pl.multiple_of(at_ref[f], 16)
        here = pl.ds(pl.multiple_of(at + WINDOW, 16), share)
        to = odd_ref if f % 2 else even_ref
        grads = jnp.concatenate([q_ref[pl.ds(at, share), :], kv_ref[here, :]], axis=1)
        to[f // 2, :, width:] = dot(grads, w_ref[:, : 3 * cols], ((1,), (1,))).astype(bf16)
        to[f // 2, :, :width] = dot(
            kv_ref[pl.ds(at, share), :], w_ref[:, cols : 3 * cols], ((1,), (1,))
        ).astype(bf16)


def rows_kernel(parts, at_ref, q_ref, kv_ref, w_ref, even_ref, odd_ref):
    cols, width = q_ref.shape[1], w_ref.shape[0]
    share = even_ref.shape[1]
    for f in range(parts):
        at = pl.multiple_of(at_ref[f], 16)
        here = pl.ds(pl.multiple_of(at + WINDOW, 16), share)
        to = odd_ref if f % 2 else even_ref
        grads = jnp.concatenate([q_ref[pl.ds(at, share), :], kv_ref[here, :]], axis=1)
        to[f // 2, :, width:] = dot(grads, w_ref[:, : 3 * cols], ((1,), (1,))).astype(bf16)
        to[f // 2, :, :width] = dot(
            kv_ref[pl.ds(at, share), :], w_ref[:, cols : 3 * cols], ((1,), (1,))
        ).astype(bf16)


def share_kernel(counts, at_ref, *refs):
    peers = len(counts)
    ctx, refs = refs[:peers], refs[peers:]
    mats = [refs[sum(counts[:r]) : sum(counts[: r + 1])] for r in range(peers)]
    refs = refs[sum(counts) :]
    x_ref, cot_ref, gain_ref = refs[:3]
    outs = refs[3:]
    res_ref, gmid_ref, part_ref, rows_ref, even_ref, odd_ref = outs[:6]
    gctx = outs[6 : 6 + peers]
    w_out, w_in, w_back = outs[6 + peers :]
    cols = ctx[0].shape[1]
    for r, pieces in enumerate(mats):
        for i, (m, k) in enumerate((m, k) for m in pieces for k in range(m.shape[0])):
            at = pl.ds(pl.multiple_of(at_ref[i], 16), m.shape[1])
            for j, w in enumerate((w_out, w_in, w_back)):
                w[at, r * cols : (r + 1) * cols] = m[k, :, j * cols : (j + 1) * cols]
    gain = gain_ref[...]
    mixed = jnp.concatenate([c[...] for c in ctx], axis=1)
    mid = x_ref[...].astype(f32) + dot(mixed, w_out[...], ((1,), (1,)))
    factor = lax.rsqrt(jnp.mean(mid * mid, axis=-1, keepdims=True) + EPSILON)
    normed = mid * factor
    h2 = (normed * gain).astype(bf16)
    rows_ref[1] = h2
    cot = cot_ref[...]
    pre = dot(h2, w_in[...], ((1,), (0,)))
    g_hid = dot(cot, w_back[...], ((1,), (0,)))
    sig = 1.0 / (1.0 + jnp.exp(-pre))
    hidden = (pre * sig).astype(bf16)
    g_pre = (g_hid * sig * (1.0 + pre * (1.0 - sig))).astype(bf16)
    for r in range(peers):
        half, to = odd_ref if r % 2 else even_ref, slice(r // 2 * cols, (r // 2 + 1) * cols)
        half[0, :, to] = g_pre[:, r * cols : (r + 1) * cols]
        half[1, :, to] = hidden[:, r * cols : (r + 1) * cols]
    res_ref[...] = mid + dot(hidden, w_back[...], ((1,), (1,)))
    g_h2 = dot(g_pre, w_in[...], ((1,), (1,)))
    part_ref[...] = jnp.sum(g_h2 * normed, axis=0, keepdims=True)
    scaled = g_h2 * gain
    back = factor * (scaled - normed * jnp.mean(scaled * normed, axis=-1, keepdims=True))
    g_mid = cot.astype(f32) + back
    gmid_ref[...] = g_mid
    gm = g_mid.astype(bf16)
    rows_ref[0] = gm
    g_mixed = dot(gm, w_out[...], ((1,), (0,))).astype(bf16)
    for r, out in enumerate(gctx):
        out[...] = g_mixed[:, r * cols : (r + 1) * cols]


def share_grads_kernel(count, at_ref, *refs):
    ctx, ctx_far = refs[:count], refs[count]
    rows_ref, rows_far, even_ref, odd_far, cot_ref, cot_far = refs[count + 1 : count + 7]
    firsts, send_ref, keep_ref = refs[count + 7 : 2 * count + 7], *refs[2 * count + 7 :]
    lefts = [
        jnp.concatenate([one.T, two.T], axis=1)
        for one, two in (
            (rows_ref[0], rows_far[0]),
            (rows_ref[1], rows_far[1]),
            (cot_ref[...], cot_far[...]),
        )
    ]
    half, cols = firsts[0].shape[-1], ctx[0].shape[1]
    zeros = jnp.zeros((firsts[0].shape[0], 2 * half - 3 * cols), bf16)
    pairs, rows = send_ref.shape[1:3]
    for r in range(count):
        to = slice(r * cols, (r + 1) * cols)
        rights = (
            (ctx[r][...], ctx_far[:, to]),
            (even_ref[0, :, to], odd_far[0, :, to]),
            (even_ref[1, :, to], odd_far[1, :, to]),
        )
        parts = [
            dot(left, jnp.concatenate(right, axis=0), ((1,), (0,))).astype(bf16)
            for left, right in zip(lefts, rights)
        ]
        whole = jnp.concatenate([*parts, zeros], axis=1)
        firsts[r][...] = whole[:, :half]
        for bit, (zero, one) in enumerate(((keep_ref, send_ref), (send_ref, keep_ref))):

            @pl.when(at_ref[0] == bit)
            def _():
                for i in range(pairs):
                    zero[r, i] = whole[2 * i * rows : (2 * i + 1) * rows, half:]
                    one[r, i] = whole[(2 * i + 1) * rows : (2 * i + 2) * rows, half:]


def grads_kernel(keep_w, came_w, keep_m, came_m, qkv_ref, out_ref, mlp_ref, col_ref, row_ref):
    cols = out_ref.shape[1]
    col_ref[...] = jnp.zeros_like(col_ref)
    row_sums = []
    for i, (keep, came) in enumerate(((keep_w, came_w), (keep_m, came_m))):
        total = keep[...].astype(f32) + came[...].astype(f32)
        for j in range(3):
            grad = total[:, j * cols : (j + 1) * cols]
            if i == 0:
                qkv_ref[j] = grad
            elif j == 0:
                out_ref[...] = grad
            else:
                mlp_ref[j - 1] = grad
            square = grad * grad
            col_ref[3 * i + j : 3 * i + j + 1, :] = jnp.sum(square, axis=0, keepdims=True)
            row_sums.append(jnp.sum(square, axis=1, keepdims=True))
    zeros = jnp.zeros((row_sums[0].shape[0], LANES - 6), f32)
    row_ref[...] = jnp.concatenate([*row_sums, zeros], axis=1).T[:8, :]


def update_kernel(sizes, qkv_ref, out_ref, mlp_ref, col_ref, row_ref, cs_ref, rs_ref, cn_ref, rn_ref, sq_ref):
    total_cols, width = sizes
    col_new = BETA_TWO * cs_ref[...] + (1.0 - BETA_TWO) * col_ref[:6, :] / width
    row_new = BETA_TWO * rs_ref[...] + (1.0 - BETA_TWO) * row_ref[:6, :] / total_cols
    cn_ref[...] = col_new
    rn_ref[...] = row_new
    rows = row_new.shape[1]
    row_cols = jnp.concatenate([row_new, jnp.ones((2, rows), f32)], axis=0).T
    sq_ref[...] = jnp.zeros_like(sq_ref)
    for i in range(6):
        grad = qkv_ref[i] if i < 3 else out_ref[...] if i == 3 else mlp_ref[i - 4]
        update = grad * lax.rsqrt(row_cols[:, i : i + 1] * col_new[i : i + 1, :])
        sq_ref[i : i + 1, :] = jnp.sum(update * update, axis=0, keepdims=True)


def step_kernel(step_ref, cn_ref, rn_ref, g_qkv, g_out, g_mlp, qkv_ref, out_ref, mlp_ref, qkv_new, out_new, mlp_new):
    rows = rn_ref.shape[1]
    row_cols = jnp.concatenate([rn_ref[...], jnp.ones((2, rows), f32)], axis=0).T
    for i in range(6):
        grad = g_qkv[i] if i < 3 else g_out[...] if i == 3 else g_mlp[i - 4]
        update = grad * lax.rsqrt(row_cols[:, i : i + 1] * cn_ref[i : i + 1, :])
        change = step_ref[i : i + 1, :] * update
        old, new = (qkv_ref, qkv_new) if i < 3 else (mlp_ref, mlp_new)
        if i == 3:
            out_new[...] = out_ref[...] - change
        else:
            new[i % 4] = old[i % 4] - change


def shards(
    tokens,
    cotangent,
    lengths,
    qkv,
    out_proj,
    mlp,
    gains,
    query_scale,
    row_second,
    col_second,
    gain_second,
    scale_second,
):
    n_tensor, n_seq = lax.axis_size("tensor"), lax.axis_size("seq")
    seq_index, ten_index = lax.axis_index("seq"), lax.axis_index("tensor")
    tok_dev, width = tokens.shape
    share = cotangent.shape[0]
    rows_own, cols_own = qkv.shape[1], qkv.shape[2]
    heads = cols_own // HD
    row_first = ten_index * share
    flips = list(range(n_tensor))
    sds = jax.ShapeDtypeStruct

    x_share = lax.dynamic_slice_in_dim(tokens, row_first, share, 0)

    padded = -(-3 * cols_own // 256) * 256
    fill = jnp.zeros((rows_own, padded - 3 * cols_own), f32)
    shard_m = jnp.concatenate([out_proj, mlp[0], mlp[1], fill], axis=1).astype(bf16)
    shard_qkv = jnp.concatenate([qkv[0], qkv[1], qkv[2], fill], axis=1).astype(bf16)
    near, far, flips_q = gather_groups(shard_qkv)
    rim_own = lax.ppermute(x_share, "seq", [(i, i + 1) for i in range(n_seq - 1)])
    rims = [rim_own] + [hop(rim_own, "tensor", f) for f in flips[2::2]]
    flips_rim = flips[::2] + flips[1::2]
    rims = rims + [hop(piece, "tensor", 1) for piece in rims]
    across = {f: {} for f in flips[2::2]}

    def send_across(g, pairs, *earlier):
        for f in across:
            across[f][g] = hop(after(pairs[g], *earlier), "tensor", f)
        return [across[f][g] for f in across]

    other_m = hop(after(shard_m, far[0]), "seq", 1)
    own_across = {f: hop(shard_m, "tensor", f) for f in across}

    def second(f, pairs):
        if not f:
            for g in across:
                across[g][0] = in_order(own_across[g], hop(other_m, "tensor", g))
            return near[-1], far[1]
        return send_across(f, pairs, rims[: n_tensor // 2])

    pairs_m = gather_pairs(shard_m, other_m, (near[1], far[0], list(own_across.values())), second)
    for g in pairs_m:
        if g % 2:
            send_across(g, pairs_m, list(across[flips[2]].values())[-1])
    flips_m = list(pairs_m)
    mats = {0: [jnp.stack([pairs_m[g] for g in flips_m])]}
    mats[1] = [hop(mats[0][0], "tensor", 1)]
    for f in across:
        mats[f] = [across[f][g][None] for g in flips_m]
    low, outer = seq_index % 2, seq_index // 2
    spots_share = [(ten_index ^ f) * share for f in flips]
    spots_q = [(outer ^ f) * 2 * rows_own for f in flips_q]
    spots_rim = [(ten_index ^ f) * share for f in flips_rim]
    spots_m = [(outer ^ f) * 2 * rows_own for f in flips_m]

    places = seq_index * tok_dev + jnp.arange(tok_dev, dtype=jnp.int32)
    ends = jnp.cumsum(lengths[0])
    passed = ends[None, :] <= places[:, None]
    doc_start = jnp.max(jnp.where(passed, ends[None, :], 0), axis=1)
    lo = jnp.maximum(places - (WINDOW - 1), doc_start)
    lo = jnp.where(places >= ends[-1], places, lo)
    lo = (lo - (seq_index * tok_dev - WINDOW)).astype(jnp.int32)[None, :]

    factor = jax.nn.softplus(query_scale) * SCALE_ROOT
    scale_cols = jnp.tile(factor, heads)[None, :]
    table = WINDOW + tok_dev
    pair_flops = tok_dev * SPAN * cols_own * 2
    stages = [pltpu.VMEM(part.shape, bf16) for part in (*near, *far)]
    n_in = len(stages) + 1 + len(rims)
    h_all, queries, key_rows, value_rows, w_qkv, log_totals, *ctx = vmem_call(
        functools.partial(attend_kernel, heads, (len(near), len(rims), n_tensor)),
        (
            sds((table, width), bf16),
            sds((tok_dev, cols_own), bf16),
            sds((table, cols_own), bf16),
            sds((table, cols_own), bf16),
            sds((width, padded), bf16),
            sds((heads, tok_dev), f32),
            *[sds((share, cols_own), bf16) for _ in flips],
        ),
        [
            pltpu.VMEM((table, width), bf16),
            pltpu.VMEM((table, width), bf16),
            pltpu.VMEM((width, padded), bf16),
            pltpu.VMEM((tok_dev, cols_own), bf16),
            pltpu.VMEM((table, cols_own), bf16),
            pltpu.VMEM((table, cols_own), bf16),
            pltpu.VMEM((heads, table, LANES), bf16),
            pltpu.VMEM((cols_own, table), bf16),
            pltpu.VMEM((2, SPAN, BLOCK), f32),
            pltpu.VMEM((tok_dev, cols_own), bf16),
            *stages,
            pltpu.SemaphoreType.DMA((n_in,)),
            pltpu.SemaphoreType.DMA((5,)),
        ],
        2 * table * width * 3 * cols_own + 6 * pair_flops,
        56,
        jnp.stack([low, *spots_q, *spots_rim, *spots_share]),
        tokens,
        *rims,
        *near,
        *far,
        gains[:1],
        scale_cols,
        lo,
        far_in=range(1, 1 + n_in),
        far_out=range(5),
    )
    for f in flips[2::2]:
        mats[f + 1] = [hop(after(piece, log_totals), "tensor", 1) for piece in mats[f]]

    ctx = [ctx[0]] + [hop(ctx[f], "tensor", f) for f in flips[1:]]
    shape_share = (share, width)
    outs = vmem_call(
        functools.partial(share_kernel, [len(mats[f]) for f in flips]),
        (
            sds(shape_share, f32),
            sds(shape_share, f32),
            sds((1, width), f32),
            sds((2, share, width), bf16),
            sds((2, share, n_tensor // 2 * cols_own), bf16),
            sds((2, share, n_tensor // 2 * cols_own), bf16),
            *[sds((share, cols_own), bf16) for _ in flips],
        ),
        [pltpu.VMEM((width, width), bf16) for _ in range(3)],
        2 * 6 * share * width * width,
        44,
        jnp.stack(spots_m),
        *ctx,
        *[piece for f in flips for piece in mats[f]],
        x_share,
        cotangent,
        gains[1:],
    )
    result, grad_mid, gain_two_grad, rows_two, even, odd = outs[:6]
    gctx = outs[6:]
    gctx = [gctx[0]] + [hop(gctx[f], "tensor", f) for f in flips[1:]]

    n_even, half = n_tensor // 2, padded // 2
    halves = sds((n_even, n_seq // 4, 2 * rows_own, half), bf16)
    *firsts, send, keep = vmem_call(
        functools.partial(share_grads_kernel, n_even),
        (*[sds((width, half), bf16) for _ in range(n_even)], halves, halves),
        [],
        2 * 3 * share * width * width,
        44,
        (outer % 2)[None],
        *ctx[::2],
        hop(jnp.concatenate(ctx[1::2], axis=1), "tensor", 1),
        rows_two,
        hop(rows_two, "tensor", 1),
        even,
        hop(odd, "tensor", 1),
        cotangent,
        hop(cotangent, "tensor", 1),
    )
    came = [hop(part, "tensor", 2 * i) for i, part in enumerate(firsts) if i]
    turned = hop(send, "seq", 2)
    log_totals, _ = lax.optimization_barrier((log_totals, firsts + [send]))

    grad_q, grad_kv, scale_raw, *grad_w = vmem_call(
        functools.partial(attend_back_kernel, heads, n_tensor),
        (
            sds((tok_dev, cols_own), bf16),
            sds((table, 2 * cols_own), bf16),
            sds((1, cols_own), f32),
            *[sds((n_seq // 2, rows_own, padded), bf16) for _ in range(2)],
        ),
        [
            pltpu.VMEM((heads, table, LANES), bf16),
            pltpu.VMEM((heads, table, LANES), bf16),
            pltpu.VMEM((cols_own, table), bf16),
            pltpu.VMEM((width, table), bf16),
            pltpu.VMEM((tok_dev, cols_own), bf16),
            pltpu.VMEM((heads, table, LANES), f32),
            pltpu.VMEM((heads, table, LANES), f32),
            pltpu.VMEM((2, SPAN, BLOCK), f32),
            pltpu.VMEM((table, width), bf16),
            pltpu.SemaphoreType.DMA,
        ],
        14 * pair_flops + 2 * table * width * 3 * cols_own,
        56,
        jnp.stack([low, *spots_share]),
        *gctx,
        queries,
        key_rows,
        value_rows,
        scale_cols,
        lo,
        log_totals,
        h_all,
        far_in=[n_tensor + 7],
    )
    scale_part = (
        jnp.sum((scale_raw / scale_cols).reshape(heads, HD), axis=0)
        * SCALE_ROOT
        * jax.nn.sigmoid(query_scale)
    )
    bits = n_seq.bit_length() - 1
    part_rows = sds((n_even, share, 2 * width), bf16)
    even_rows, odd_rows = vmem_call(
        functools.partial(rows_kernel, n_tensor),
        (part_rows, part_rows),
        [],
        2 * (tok_dev * 5 * cols_own) * width,
        44,
        jnp.stack(spots_share),
        grad_q,
        grad_kv,
        w_qkv,
    )
    turned_w = hop(grad_w[0], "seq", 1)

    first = firsts[0].astype(f32)
    for part in came:
        first = first + part.astype(f32)
    first = first.reshape(*[2] * bits, rows_own, half)
    send, keep_first = scatter_step(first, list(range(bits)), 1)
    second = keep.astype(f32) + turned.astype(f32)
    sends = [second[i].astype(bf16) for i in range(1, n_even)]
    came_first = hop(send, "seq", 2)
    far_second = [hop(part, "tensor", 2 * i + 2) for i, part in enumerate(sends)]
    from_core_rows = hop(after(odd_rows, turned_w, came_first, far_second), "tensor", 1)
    sums = [even_rows[i].astype(f32) + from_core_rows[i].astype(f32) for i in range(n_even)]
    sum_sends = [part.astype(bf16) for part in sums[1:]]

    parts_m, rest = [], [0, *range(2, bits)]
    first = keep_first + came_first.astype(f32)
    second = second[0]
    for part in far_second:
        second = second + part.astype(f32)
    second = second.reshape(*[2] * (bits - 1), rows_own, half)
    for part, left, order in (
        (first, rest, rest),
        (second, rest, rest[::-1]),
    ):
        parts_m.append(scatter_seq(part, left, order))
    sum_sends = after(sum_sends, turned_w, far_second)
    far_rim = [hop(part[:, :width], "tensor", 2 * i + 2) for i, part in enumerate(sum_sends)]
    rim_one, grad_one = sums[0][:, :width], sums[0][:, width:]
    for part in far_rim:
        rim_one = rim_one + part.astype(f32)
    far_here = [
        hop(after(part[:, width:], far_rim), "tensor", 2 * i + 2)
        for i, part in enumerate(sum_sends)
    ]
    for part in far_here:
        grad_one = grad_one + part.astype(f32)
    high = list(range(1, bits))
    own_qkv = grad_w[1].astype(f32) + turned_w.astype(f32)
    own_qkv = own_qkv.reshape(*[2] * (bits - 1), *own_qkv.shape[1:])
    send, keep_w = scatter_step(own_qkv, high, 1)
    came_w = hop(send, "seq", 2)
    keep_m, came_m = (jnp.concatenate(part, axis=1) for part in zip(*parts_m))
    if bits > 2:
        own_qkv = keep_w.astype(f32) + came_w.astype(f32)
        keep_w, came_w = scatter_seq(own_qkv, high[1:], high[1:])
    cut = (width // 512) * 128
    to_last = [(i, i - 1) for i in range(1, n_seq)]
    rim_low = rim_one.astype(bf16)
    back = [lax.ppermute(part, "seq", to_last) for part in (rim_low[:, :cut], rim_low[:, cut:])]
    grad_one = grad_one + jnp.concatenate(back, axis=1).astype(f32)
    came_w = after(came_w, back[0], far_here)
    x_part = x_share.astype(f32)
    factor_one = lax.rsqrt(jnp.mean(x_part * x_part, axis=-1, keepdims=True) + EPSILON)
    norm_one = x_part * factor_one
    gain_one_grad = jnp.sum(grad_one * norm_one, axis=0)
    scaled = grad_one * gains[0]
    tokens_grad = grad_mid + factor_one * (
        scaled - norm_one * jnp.mean(scaled * norm_one, axis=-1, keepdims=True)
    )

    total_cols = cols_own * n_tensor
    shape_w = (sds((3, rows_own, cols_own), f32), sds((rows_own, cols_own), f32))
    shape_w = (*shape_w, sds((2, rows_own, cols_own), f32))
    *grads, col_part, row_part = vmem_call(
        grads_kernel,
        (*shape_w, sds((8, cols_own), f32), sds((8, rows_own), f32)),
        [],
        1e9,
        32,
        keep_w,
        came_w,
        keep_m,
        came_m,
    )
    col_new, row_new, unscaled_part = vmem_call(
        functools.partial(update_kernel, (total_cols, width)),
        (
            sds((6, cols_own), f32),
            sds((6, rows_own), f32),
            sds((6, cols_own), f32),
        ),
        [],
        1e9,
        32,
        *grads,
        after(summed(col_part, "seq"), back),
        summed(row_part, "tensor"),
        col_second,
        row_second,
    )

    gain_part = jnp.stack([gain_one_grad, gain_two_grad[0]])
    gain_part = gain_part.reshape(2, n_seq, rows_own).transpose(1, 0, 2).reshape(n_seq, 2 * rows_own)
    rest = jnp.concatenate(
        [
            scale_part,
            jnp.sum(unscaled_part, axis=1),
            jnp.sum(row_part[:6], axis=1),
            jnp.sum(row_second, axis=1) / n_tensor,
        ]
    )
    rest = jnp.broadcast_to(rest, (n_seq, HD + 18))
    last = jnp.concatenate([gain_part, rest], axis=1)
    size = -(-last.shape[1] // 1024) * 1024
    last = jnp.pad(last, ((0, 0), (0, size - last.shape[1]))).reshape(n_seq, 1, size // 128, 128)
    last = jnp.broadcast_to(last, (n_seq, n_tensor, size // 128, 128))
    last = last.reshape(n_seq * n_tensor, size // 128, 128)
    got = lax.all_to_all(last, ("seq", "tensor"), split_axis=0, concat_axis=0)
    gains_grad, scale_grad, unscaled_square, all_square, old_sums = unpacked(
        jnp.sum(got, axis=0), (2, rows_own), (HD,), (6,), (6,), (6,)
    )
    row_mean = (BETA_TWO * old_sums + (1.0 - BETA_TWO) * all_square / total_cols) / width
    update_rms = jnp.sqrt(row_mean * unscaled_square / (width * total_cols))
    step = STEP_RATE * jnp.sqrt(row_mean) / jnp.maximum(1.0, update_rms / CLIP_LEVEL)
    fresh = vmem_call(
        step_kernel,
        shape_w,
        [],
        1e9,
        32,
        jnp.broadcast_to(step[:, None], (6, cols_own)),
        col_new,
        row_new,
        *grads,
        qkv,
        out_proj,
        mlp,
    )
    gains_own = lax.dynamic_slice_in_dim(gains, seq_index * rows_own, rows_own, 1)
    gain_second_new = BETA_TWO * gain_second + (1.0 - BETA_TWO) * gains_grad * gains_grad
    gains_new = gains_own - VECTOR_RATE * gains_grad * lax.rsqrt(gain_second_new)
    scale_second_new = BETA_TWO * scale_second + (1.0 - BETA_TWO) * scale_grad * scale_grad
    scale_new = query_scale - VECTOR_RATE * scale_grad * lax.rsqrt(scale_second_new)
    return (
        result,
        tokens_grad,
        *grads,
        gains_grad,
        scale_grad,
        *fresh,
        gains_new,
        scale_new,
        row_new,
        col_new,
        update_rms,
        gain_second_new,
        scale_second_new,
    )


def solution(mesh):
    return jax.shard_map(
        shards,
        mesh=mesh,
        in_specs=(
            P("seq", None),
            P(("seq", "tensor"), None),
            P(),
            P(None, "seq", "tensor"),
            P("seq", "tensor"),
            P(None, "seq", "tensor"),
            P(),
            P(),
            P(None, "seq"),
            P(None, "tensor"),
            P(None, "seq"),
            P(),
        ),
        out_specs=(
            P(("seq", "tensor"), None),
            P(("seq", "tensor"), None),
            P(None, "seq", "tensor"),
            P("seq", "tensor"),
            P(None, "seq", "tensor"),
            P(None, "seq"),
            P(),
            P(None, "seq", "tensor"),
            P("seq", "tensor"),
            P(None, "seq", "tensor"),
            P(None, "seq"),
            P(),
            P(None, "seq"),
            P(None, "tensor"),
            P(),
            P(None, "seq"),
            P(),
        ),
        check_vma=False,
    )
```
